32 devices in a mesh: space: 4 (over y, x), species: 8 (over z, core).
Axes of the slice: x: 2, y: 2, z: 4, core: 2. Of those that a mesh axis runs over, the one named last changes fastest.
Arguments:
- dust_state: float32 [3, 32, 128, 1024], P(None, 'species', 'space'), may hold values from -4 to 4, as said below
- gas_state: float32 [3, 128, 1024], P(None, 'space'), may hold values from -2 to 2, as said below
- species_bin: int32 [32], P('species'), may hold values from 0 to 31, each once
Outputs:
- dust_out: float32 [3, 32, 128, 1024], P(None, 'species', 'space')
- gas_out: float32 [3, 128, 1024], P(None, 'space')
The draws below stay inside these ranges and needn't reach their ends.
Inputs may be any that keep to these rules, and one draw needn't show every extreme that they name: `dust_state`: component 0 (densities) lies in 0.5 to 2; the velocities lie within -4 to 4. `gas_state`: component 0 (density) lies in 0.5 to 2; the velocities lie within -2 to 2.
All inputs are finite; a program needn't handle non-finite values.
Results may differ from the reference program's by a relative error of at most 0.0003.
Values sent between devices are 32-bit elements; how exact they have to be, the bound alone decides.
A program may use at most 64 MiB of HBM per device.

```python
import math
import jax
import jax.numpy as jnp
from jax import lax

NR = 1024
STEPS = 2
NSP = 32
NA = 128


def draw_dust_state(key, part):
    key_density, key_motion = jax.random.split(jax.random.fold_in(key, 11))
    density = jnp.exp(jax.random.uniform(key_density, (1, NSP, NA, NR), jnp.float32, math.log(0.5), math.log(2.0)))
    motion = jax.random.truncated_normal(key_motion, -4.0, 4.0, (2, NSP, NA, NR), jnp.float32)
    return jnp.concatenate([density, motion], axis=0)


def draw_gas_state(key, part):
    key_density, key_motion = jax.random.split(jax.random.fold_in(key, 23))
    density = jnp.exp(jax.random.uniform(key_density, (1, NA, NR), jnp.float32, math.log(0.5), math.log(2.0)))
    motion = 0.5 * jax.random.truncated_normal(key_motion, -4.0, 4.0, (2, NA, NR), jnp.float32)
    return jnp.concatenate([density, motion], axis=0)


def setup_inputs(seed: int = 0) -> dict:
    streams_of = jax.random.split(jax.random.key(seed), 4)
    return {
        "dust_state": draw_dust_state(jax.random.fold_in(streams_of[3], 71), 0),
        "gas_state": draw_gas_state(jax.random.fold_in(streams_of[3], 71), 0),
        "species_bin": jax.random.permutation(streams_of[2], NSP).astype(jnp.int32),
    }


courant = 0.25
sound_speed = 1.0
sound_sq = 1.0
stop_floor = 0.003
stop_span = 6.907755


def window(values, start, length, along):
    return lax.slice_in_dim(values, start, start + length, axis=along)


def face_divergence(density, velocity, along):
    faces = density.shape[along] - 3
    back_two = window(density, 0, faces, along)
    here = window(density, 1, faces, along)
    ahead = window(density, 2, faces, along)
    ahead_two = window(density, 3, faces, along)
    face_speed = 0.5 * (window(velocity, 1, faces, along) + window(velocity, 2, faces, along))
    flux = jnp.maximum(face_speed, 0.0) * (1.5 * here - 0.5 * back_two) + jnp.minimum(face_speed, 0.0) * (1.5 * ahead - 0.5 * ahead_two)
    return window(flux, 1, faces - 1, along) - window(flux, 0, faces - 1, along)


def moved(fluid, step_time):
    density = fluid[0]
    radial = fluid[1]
    azimuth = fluid[2]
    div_azimuth = face_divergence(density, azimuth, 1)
    inner_density = density[:, 2:-2]
    inner_radial = radial[:, 2:-2]
    zero_pad = ((0, 0), (0, 0), (2, 2))
    div_radial = face_divergence(jnp.pad(inner_density, zero_pad), jnp.pad(inner_radial, zero_pad), 2)
    new_density = inner_density - step_time * (div_azimuth + div_radial)
    gas_density = density[-1]
    inner_gas = gas_density[2:-2]
    grad_azimuth = 0.5 * (gas_density[3:-1] - gas_density[1:-3])
    edge_gas = jnp.pad(inner_gas, ((0, 0), (1, 1)), mode="edge")
    grad_radial = 0.5 * (edge_gas[:, 2:] - edge_gas[:, :-2])
    push = step_time * sound_sq / inner_gas
    gas_velocity = jnp.stack([inner_radial[-1] - push * grad_radial, azimuth[-1, 2:-2] - push * grad_azimuth])
    dust_velocity = jnp.stack([inner_radial[:-1], azimuth[:-1, 2:-2]])
    return new_density, gas_velocity, dust_velocity


def drag_terms(new_density, dust_velocity, stop_times, step_time, total_species):
    gas_new = new_density[-1]
    rate = step_time * gas_new[None] / stop_times[:, None, None]
    weight = new_density[:-1] / (total_species * gas_new[None]) * rate / (1.0 + rate)
    terms = jnp.stack([jnp.sum(weight, 0), jnp.sum(weight * dust_velocity[0], 0), jnp.sum(weight * dust_velocity[1], 0)])
    return rate, terms


def coupled_gas(gas_velocity, totals):
    return (gas_velocity + totals[1:]) / (1.0 + totals[0])


def assemble(new_density, dust_velocity, gas_next, rate):
    dust_next = (dust_velocity + rate[None] * gas_next[:, None]) / (1.0 + rate[None])
    radial = jnp.concatenate([dust_next[0], gas_next[0][None]], axis=0)
    azimuth = jnp.concatenate([dust_next[1], gas_next[1][None]], axis=0)
    return jnp.stack([new_density, radial, azimuth])


def reference(dust_state, gas_state, species_bin):
    fluid = jnp.concatenate([dust_state, gas_state[:, None]], axis=1)
    stop_times = stop_floor * jnp.exp(stop_span * species_bin.astype(jnp.float32) / (NSP - 1))
    for iteration in range(STEPS):
        speeds = jnp.abs(fluid[1]) + jnp.abs(fluid[2])
        step_time = courant / (sound_speed + jnp.max(speeds))
        wide = jnp.pad(fluid, ((0, 0), (0, 0), (2, 2), (0, 0)), mode="wrap")
        new_density, gas_velocity, dust_velocity = moved(wide, step_time)
        rate, terms = drag_terms(new_density, dust_velocity, stop_times, step_time, NSP)
        gas_next = coupled_gas(gas_velocity, terms)
        fluid = assemble(new_density, dust_velocity, gas_next, rate)
    return fluid[:, :NSP], fluid[:, NSP]
```

```python
import functools

import jax
import jax.numpy as jnp
from jax import lax
from jax.experimental import pallas as pl
from jax.experimental.pallas import tpu as pltpu
from jax.sharding import PartitionSpec as P

STEPS = 2

courant = 0.25
sound_speed = 1.0
stop_floor = 0.003
stop_span = 6.907755

MESH = pl.DeviceIdType.MESH
TOP = 8


def kernel(
    n, m, dust, gas, inv_stop, dust_out, gas_out,
    rho, rad, azi, div, push, damp, terms, gnew,
    sib_recv, rs_recv, top_send, top_one, top_mid, top_two, halo_send, halo_recv,
    io_sem, top_sems, halo_sems, sib_sems, rs_sems, ag_sems, fw_sems,
):
    local_species, tile_rows, cells = dust.shape[1:]
    fluids = local_species + 1
    gas_at = local_species
    groups = tile_rows // 8
    spans = n // groups
    width = cells // spans
    chips = n // 2
    total_species = local_species * n
    bottom = TOP + tile_rows

    me_space = lax.axis_index("space")
    me = lax.axis_index("species")
    core = lax.rem(me, 2)
    chip = me // 2
    sibling = me + 1 - 2 * core
    interior = pl.ds(TOP, tile_rows)

    loads = []
    for part, held in enumerate((rho, rad, azi)):
        loads.append(pltpu.make_async_copy(
            dust.at[part], held.at[pl.ds(0, local_species), interior], io_sem.at[2 * part]))
        loads.append(pltpu.make_async_copy(
            gas.at[part], held.at[gas_at, interior], io_sem.at[2 * part + 1]))
    for load in loads:
        load.start()

    barrier = pltpu.get_barrier_semaphore()

    def greet_species(i, carry):
        pl.semaphore_signal(
            barrier, inc=1, device_id=(me_space, lax.rem(me + 1 + i, n)), device_id_type=MESH)
        return carry

    def greet_space(i, carry):
        pl.semaphore_signal(
            barrier, inc=1, device_id=(lax.rem(me_space + 1 + i, m), me), device_id_type=MESH)
        return carry

    lax.fori_loop(0, n - 1, greet_species, 0)
    lax.fori_loop(0, m - 1, greet_space, 0)
    for load in loads:
        load.wait()

    def fold(values):
        best = values[:, :128]
        for start in range(128, values.shape[1], 128):
            best = jnp.maximum(best, values[:, start:start + 128])
        return best

    def first_top(i, best):
        f = i // groups
        rows = pl.ds(pl.multiple_of(TOP + 8 * lax.rem(i, groups), 8), 8)
        return jnp.maximum(best, fold(jnp.abs(rad[f, rows, :]) + jnp.abs(azi[f, rows, :])))

    top = lax.fori_loop(0, fluids * groups, first_top, jnp.zeros((8, 128), jnp.float32))

    def copy_to(src, dst, send, recv, where):
        return pltpu.make_async_remote_copy(
            src_ref=src, dst_ref=dst, send_sem=send, recv_sem=recv,
            device_id=where, device_id_type=MESH)

    lanes = lax.broadcasted_iota(jnp.int32, (8, cells), 1)

    for step in range(STEPS):
        top_send[step] = top
        top_one[step, me] = top
        for f in range(fluids):
            for side, (far, near) in enumerate(((bottom - 2, bottom - 1), (TOP + 1, TOP))):
                halo_send[step, side, f:f + 1, :] = rho[f, far:far + 1, :]
                halo_send[step, side, fluids + f:fluids + f + 1, :] = rho[f, near:near + 1, :]
                halo_send[step, side, 2 * fluids + f:2 * fluids + f + 1, :] = azi[f, near:near + 1, :]
        if step == 0:
            pl.semaphore_wait(barrier, n + m - 2)

        def top_copy_one(i):
            there = lax.rem(me + 1 + i, n)
            return copy_to(top_send.at[step], top_one.at[step, me], top_sems.at[step, 0, i],
                           top_sems.at[step, 1, me], (me_space, there))

        def top_copy_two(i):
            there = lax.rem(me_space + 1 + i, m)
            return copy_to(top_mid.at[step], top_two.at[step, me_space], top_sems.at[step, 2, i],
                           top_sems.at[step, 3, me_space], (there, me))

        def start_one(i, carry):
            top_copy_one(i).start()
            return carry

        lax.fori_loop(0, n - 1, start_one, 0)
        halos = []
        for side, there in enumerate((lax.rem(me_space + 1, m), lax.rem(me_space + m - 1, m))):
            halos.append(copy_to(halo_send.at[step, side], halo_recv.at[step, side],
                                 halo_sems.at[step, 0, side], halo_sems.at[step, 1, side],
                                 (there, me)))
        for halo in halos:
            halo.start()

        def radial(i, carry):
            f = i // groups
            r = lax.rem(i, groups)
            rows = pl.ds(pl.multiple_of(TOP + 8 * r, 8), 8)
            here = rho[f, rows, :]
            speed = rad[f, rows, :]
            back = jnp.where(lanes >= 1, pltpu.roll(here, 1, 1), 0.0)
            ahead = jnp.where(lanes < cells - 1, pltpu.roll(here, cells - 1, 1), 0.0)
            down = 3.0 * here - ahead
            down_next = jnp.where(lanes < cells - 1, pltpu.roll(down, cells - 1, 1), 0.0)
            face = speed + jnp.where(lanes < cells - 1, pltpu.roll(speed, cells - 1, 1), 0.0)
            flux = face * jnp.where(face > 0.0, 3.0 * here - back, down_next)
            before = jnp.where(lanes >= 1, pltpu.roll(flux, 1, 1), jnp.minimum(speed, 0.0) * down)
            div[f, pl.ds(pl.multiple_of(8 * r, 8), 8), :] = flux - before
            return carry

        lax.fori_loop(0, fluids * groups, radial, 0)

        def gas_push(r, carry):
            rows = pl.ds(pl.multiple_of(TOP + 8 * r, 8), 8)
            here = rho[gas_at, rows, :]
            up = jnp.where(lanes < cells - 1, pltpu.roll(here, cells - 1, 1), here)
            low = jnp.where(lanes >= 1, pltpu.roll(here, 1, 1), here)
            push[0, pl.ds(pl.multiple_of(8 * r, 8), 8), :] = (up - low) * (0.5 / here)
            return carry

        lax.fori_loop(0, groups, gas_push, 0)

        def wait_one(i, best):
            there = lax.rem(me + 1 + i, n)
            copy_to(top_send.at[step], top_one.at[step, there], top_sems.at[step, 0, i],
                    top_sems.at[step, 1, there], (me_space, there)).wait_recv()
            return jnp.maximum(best, top_one[step, there])

        top = lax.fori_loop(0, n - 1, wait_one, top)
        top_mid[step] = top

        def start_two(i, carry):
            top_copy_two(i).start()
            return carry

        lax.fori_loop(0, m - 1, start_two, 0)

        for halo in halos:
            halo.wait_recv()
        for f in range(fluids):
            for side, (far, near) in enumerate(((TOP - 2, TOP - 1), (bottom + 1, bottom))):
                rho[f, far:far + 1, :] = halo_recv[step, side, f:f + 1, :]
                rho[f, near:near + 1, :] = halo_recv[step, side, fluids + f:fluids + f + 1, :]
                azi[f, near:near + 1, :] = halo_recv[
                    step, side, 2 * fluids + f:2 * fluids + f + 1, :]

        def azimuthal(f, carry):
            for r in range(groups):
                at = TOP + 8 * r
                here = rho[f, at:at + 8, :]
                back_two = rho[f, at - 2:at + 6, :]
                back = rho[f, at - 1:at + 7, :]
                ahead = rho[f, at + 1:at + 9, :]
                ahead_two = rho[f, at + 2:at + 10, :]
                speed = azi[f, at:at + 8, :]
                low = speed + azi[f, at - 1:at + 7, :]
                high = speed + azi[f, at + 1:at + 9, :]
                after = high * jnp.where(high > 0.0, 3.0 * here - back, 3.0 * ahead - ahead_two)
                before = low * jnp.where(low > 0.0, 3.0 * back - back_two, 3.0 * here - ahead)
                div[f, 8 * r:8 * r + 8, :] += after - before
            return carry

        lax.fori_loop(0, fluids, azimuthal, 0)
        for r in range(groups):
            at = TOP + 8 * r
            push[1, 8 * r:8 * r + 8, :] = (
                rho[gas_at, at + 1:at + 9, :] - rho[gas_at, at - 1:at + 7, :]
            ) * (0.5 / rho[gas_at, at:at + 8, :])

        def wait_two(i, best):
            there = lax.rem(me_space + 1 + i, m)
            copy_to(top_mid.at[step], top_two.at[step, there], top_sems.at[step, 2, i],
                    top_sems.at[step, 3, there], (there, me)).wait_recv()
            return jnp.maximum(best, top_two[step, there])

        top = lax.fori_loop(0, m - 1, wait_two, top)
        fastest = jnp.max(jnp.max(top, axis=0, keepdims=True), axis=1, keepdims=True)
        dt = courant / (sound_speed + fastest)
        dt_quarter = 0.25 * dt

        def place(chunk):
            r = chunk // spans
            g = lax.rem(chunk, spans)
            cols = pl.ds(pl.multiple_of(width * g, 128), width)
            return (pl.ds(pl.multiple_of(TOP + 8 * r, 8), 8),
                    pl.ds(pl.multiple_of(8 * r, 8), 8), cols)

        def drag(chunk):
            rows, inner, cols = place(chunk)
            new_gas = rho[gas_at, rows, cols] - dt_quarter * div[gas_at, inner, cols]
            rho[gas_at, rows, cols] = new_gas
            sums = [jnp.zeros((8, width), jnp.float32)] * 3
            for k in range(local_species):
                scale = dt * inv_stop[k]
                new = rho[k, rows, cols] - dt_quarter * div[k, inner, cols]
                rho[k, rows, cols] = new
                factor = 1.0 / (1.0 + scale * new_gas)
                damp[k, inner, cols] = factor
                weight = (new * factor) * (scale * (1.0 / total_species))
                sums[0] = sums[0] + weight
                sums[1] = sums[1] + weight * rad[k, rows, cols]
                sums[2] = sums[2] + weight * azi[k, rows, cols]
            return sums

        def sib_copy(i):
            return copy_to(terms.at[step, 1 - core, i], sib_recv.at[step, i],
                           sib_sems.at[step, 0, i], sib_sems.at[step, 1, i], (me_space, sibling))

        def rs_copy(z):
            return copy_to(terms.at[step, core, z], rs_recv.at[step, chip],
                           rs_sems.at[step, 0, z], rs_sems.at[step, 1, chip],
                           (me_space, 2 * z + core))

        def rs_arrival(z):
            return copy_to(terms.at[step, core, z], rs_recv.at[step, z],
                           rs_sems.at[step, 0, z], rs_sems.at[step, 1, z],
                           (me_space, 2 * z + core))

        def for_sibling(i, carry):
            z = lax.rem(chip + 1 + i, chips)
            sums = drag(2 * z + 1 - core)
            for part in range(3):
                terms[step, 1 - core, z, part] = sums[part]
            sib_copy(z).start()
            return carry

        lax.fori_loop(0, chips, for_sibling, 0)

        def for_peers(i, carry):
            z = lax.rem(chip + 1 + i, chips)
            sums = drag(2 * z + core)
            sib_copy(z).wait_recv()
            for part in range(3):
                terms[step, core, z, part] = sums[part] + sib_recv[step, z, part]

            @pl.when(i < chips - 1)
            def _():
                rs_copy(z).start()

            return carry

        lax.fori_loop(0, chips, for_peers, 0)

        def gather_sums(i, sums):
            z = lax.rem(chip + 1 + i, chips)
            rs_arrival(z).wait_recv()
            return tuple(sums[part] + rs_recv[step, z, part] for part in range(3))

        sums = lax.fori_loop(
            0, chips - 1, gather_sums, tuple(terms[step, core, chip, part] for part in range(3)))

        rows, inner, cols = place(me)
        inverse = 1.0 / (1.0 + sums[0])
        gnew[step, me, 0] = (rad[gas_at, rows, cols] - dt * push[0, inner, cols] + sums[1]) * inverse
        gnew[step, me, 1] = (azi[gas_at, rows, cols] - dt * push[1, inner, cols] + sums[2]) * inverse

        def ag_copy(z):
            return copy_to(gnew.at[step, me], gnew.at[step, me], ag_sems.at[step, 0, z],
                           ag_sems.at[step, 1, chip], (me_space, 2 * z + core))

        def ag_arrival(z):
            return copy_to(gnew.at[step, 2 * z + core], gnew.at[step, 2 * z + core],
                           ag_sems.at[step, 0, z], ag_sems.at[step, 1, z],
                           (me_space, 2 * z + core))

        def fw_copy(z):
            return copy_to(gnew.at[step, 2 * z + core], gnew.at[step, 2 * z + core],
                           fw_sems.at[step, 0, z], fw_sems.at[step, 1, z], (me_space, sibling))

        def fw_arrival(z):
            other = 2 * z + 1 - core
            return copy_to(gnew.at[step, other], gnew.at[step, other],
                           fw_sems.at[step, 0, z], fw_sems.at[step, 1, z], (me_space, sibling))

        def start_ag(i, carry):
            ag_copy(lax.rem(chip + 1 + i, chips)).start()
            return carry

        lax.fori_loop(0, chips - 1, start_ag, 0)
        fw_copy(chip).start()

        def update(chunk, best):
            rows, inner, cols = place(chunk)
            gas_rad = gnew[step, chunk, 0]
            gas_azi = gnew[step, chunk, 1]
            rad[gas_at, rows, cols] = gas_rad
            azi[gas_at, rows, cols] = gas_azi
            speed = jnp.abs(gas_rad) + jnp.abs(gas_azi)
            for k in range(local_species):
                factor = damp[k, inner, cols]
                new_rad = gas_rad + (rad[k, rows, cols] - gas_rad) * factor
                new_azi = gas_azi + (azi[k, rows, cols] - gas_azi) * factor
                rad[k, rows, cols] = new_rad
                azi[k, rows, cols] = new_azi
                speed = jnp.maximum(speed, jnp.abs(new_rad) + jnp.abs(new_azi))
            return jnp.maximum(best, fold(speed))

        top = update(me, jnp.zeros((8, 128), jnp.float32))

        def update_peer(i, best):
            z = lax.rem(chip + 1 + i, chips)
            ag_arrival(z).wait_recv()
            fw_copy(z).start()
            return update(2 * z + core, best)

        top = lax.fori_loop(0, chips - 1, update_peer, top)

        def update_sibling(i, best):
            z = lax.rem(chip + i, chips)
            fw_arrival(z).wait_recv()
            return update(2 * z + 1 - core, best)

        top = lax.fori_loop(0, chips, update_sibling, top)

        def sent_one(i, carry):
            top_copy_one(i).wait_send()
            return carry

        def sent_two(i, carry):
            top_copy_two(i).wait_send()
            return carry

        def sent_core(i, carry):
            sib_copy(i).wait_send()
            fw_copy(i).wait_send()
            return carry

        def sent_chip(i, carry):
            z = lax.rem(chip + 1 + i, chips)
            rs_copy(z).wait_send()
            ag_copy(z).wait_send()
            return carry

        lax.fori_loop(0, n - 1, sent_one, 0)
        lax.fori_loop(0, m - 1, sent_two, 0)
        lax.fori_loop(0, chips, sent_core, 0)
        lax.fori_loop(0, chips - 1, sent_chip, 0)
        for halo in halos:
            halo.wait_send()

    stores = []
    for part, held in enumerate((rho, rad, azi)):
        stores.append(pltpu.make_async_copy(
            held.at[pl.ds(0, local_species), interior], dust_out.at[part], io_sem.at[2 * part]))
        stores.append(pltpu.make_async_copy(
            held.at[gas_at, interior], gas_out.at[part], io_sem.at[2 * part + 1]))
    for store in stores:
        store.start()
    for store in stores:
        store.wait()


def solution(mesh):
    n = mesh.shape["species"]
    m = mesh.shape["space"]

    def local(dust_state, gas_state, species_bin):
        local_species, tile_rows, cells = dust_state.shape[1:]
        fluids = local_species + 1
        groups = tile_rows // 8
        width = cells // (n // groups)
        chips = n // 2
        total_species = local_species * n
        inv_stop = jnp.exp(
            -stop_span * species_bin.astype(jnp.float32) / (total_species - 1)
        ) / stop_floor
        f32 = jnp.float32
        halo_rows = -(-3 * fluids // 8) * 8
        extended = pltpu.VMEM((fluids, tile_rows + 16, cells), f32)
        dma = pltpu.SemaphoreType.DMA
        return pl.pallas_call(
            functools.partial(kernel, n, m),
            out_shape=(jax.ShapeDtypeStruct(dust_state.shape, f32),
                       jax.ShapeDtypeStruct(gas_state.shape, f32)),
            in_specs=[pl.BlockSpec(memory_space=pl.ANY), pl.BlockSpec(memory_space=pl.ANY),
                      pl.BlockSpec(memory_space=pltpu.SMEM)],
            out_specs=(pl.BlockSpec(memory_space=pl.ANY), pl.BlockSpec(memory_space=pl.ANY)),
            scratch_shapes=[
                extended, extended, extended,
                pltpu.VMEM((fluids, tile_rows, cells), f32),
                pltpu.VMEM((2, tile_rows, cells), f32),
                pltpu.VMEM((local_species, tile_rows, cells), f32),
                pltpu.VMEM((STEPS, 2, chips, 3, 8, width), f32),
                pltpu.VMEM((STEPS, n, 2, 8, width), f32),
                pltpu.VMEM((STEPS, chips, 3, 8, width), f32),
                pltpu.VMEM((STEPS, chips, 3, 8, width), f32),
                pltpu.VMEM((STEPS, 8, 128), f32),
                pltpu.VMEM((STEPS, n, 8, 128), f32),
                pltpu.VMEM((STEPS, 8, 128), f32),
                pltpu.VMEM((STEPS, m, 8, 128), f32),
                pltpu.VMEM((STEPS, 2, halo_rows, cells), f32),
                pltpu.VMEM((STEPS, 2, halo_rows, cells), f32),
                dma((6,)),
                dma((STEPS, 4, max(n, m))),
                dma((STEPS, 2, 2)),
                dma((STEPS, 2, chips)),
                dma((STEPS, 2, chips)),
                dma((STEPS, 2, chips)),
                dma((STEPS, 2, chips)),
            ],
            compiler_params=pltpu.CompilerParams(
                collective_id=0, has_side_effects=True, vmem_limit_bytes=56 * 1024 * 1024),
            cost_estimate=pl.CostEstimate(
                flops=200 * fluids * tile_rows * cells,
                bytes_accessed=24 * fluids * tile_rows * cells, transcendentals=0),
            name="disk_steps",
        )(dust_state, gas_state, inv_stop)

    return jax.shard_map(
        local,
        mesh=mesh,
        in_specs=(P(None, "species", "space", None), P(None, "space", None), P("species")),
        out_specs=(P(None, "species", "space", None), P(None, "space", None)),
        check_vma=False,
    )
```

```python
import functools

import jax
import jax.numpy as jnp
from jax import lax
from jax.experimental import pallas as pl
from jax.experimental.pallas import tpu as pltpu
from jax.sharding import PartitionSpec as P

STEPS = 2

courant = 0.25
sound_speed = 1.0
stop_floor = 0.003
stop_span = 6.907755

MESH = pl.DeviceIdType.MESH
TOP = 8


def kernel(
    n, m, dust, gas, species_bins, rho, rad, azi, damp,
    species_bin, div, push, terms, gnew,
    sib_recv, rs_recv, top_send, top_one, top_mid, top_two, halo_send, halo_recv,
    io_sem, top_sems, halo_sems, sib_sems, rs_sems, ag_sems, fw_sems,
):
    local_species, tile_rows, cells = dust.shape[1:]
    fluids = local_species + 1
    gas_at = local_species
    groups = tile_rows // 8
    spans = n // groups
    width = cells // spans
    chips = n // 2
    total_species = local_species * n
    bottom = TOP + tile_rows

    me_space = lax.axis_index("space")
    me = lax.axis_index("species")
    core = lax.rem(me, 2)
    chip = me // 2
    sibling = me + 1 - 2 * core
    interior = pl.ds(TOP, tile_rows)

    barrier = pltpu.get_barrier_semaphore()

    def greet_species(i, carry):
        pl.semaphore_signal(
            barrier, inc=1, device_id=(me_space, lax.rem(me + 1 + i, n)), device_id_type=MESH)
        return carry

    def greet_space(i, carry):
        pl.semaphore_signal(
            barrier, inc=1, device_id=(lax.rem(me_space + 1 + i, m), me), device_id_type=MESH)
        return carry

    lax.fori_loop(0, n - 1, greet_species, 0)
    lax.fori_loop(0, m - 1, greet_space, 0)
    loads = []
    for part, held in enumerate((rho, rad, azi)):
        loads.append(pltpu.make_async_copy(
            dust.at[part], held.at[pl.ds(0, local_species), interior], io_sem.at[2 * part]))
        loads.append(pltpu.make_async_copy(
            gas.at[part], held.at[gas_at, interior], io_sem.at[2 * part + 1]))
    loads.append(pltpu.make_async_copy(species_bins, species_bin, io_sem.at[6]))
    for load in loads:
        load.start()
    for load in loads:
        load.wait()

    def fold(values):
        best = values[:, :128]
        for start in range(128, values.shape[1], 128):
            best = jnp.maximum(best, values[:, start:start + 128])
        return best

    def first_top(i, best):
        f = i // groups
        rows = pl.ds(pl.multiple_of(TOP + 8 * lax.rem(i, groups), 8), 8)
        return jnp.maximum(best, fold(jnp.abs(rad[f, rows, :]) + jnp.abs(azi[f, rows, :])))

    top = lax.fori_loop(0, fluids * groups, first_top, jnp.zeros((8, 128), jnp.float32))

    def copy_to(src, dst, send, recv, where):
        return pltpu.make_async_remote_copy(
            src_ref=src, dst_ref=dst, send_sem=send, recv_sem=recv,
            device_id=where, device_id_type=MESH)

    inv_stop = [
        jnp.exp(jnp.full((1, 1), species_bin[k].astype(jnp.float32))
                * (-stop_span / (total_species - 1))) * (1.0 / stop_floor)
        for k in range(local_species)]
    lanes = lax.broadcasted_iota(jnp.int32, (8, cells), 1)

    unsent = []

    def run_step(step, top):
        top_send[step] = top
        if step == 0:
            pl.semaphore_wait(barrier, n + m - 2)

        def top_copy_one(i):
            there = lax.rem(me + 1 + i, n)
            return copy_to(top_send.at[step], top_one.at[step, me], top_sems.at[step, 0, i],
                           top_sems.at[step, 1, me], (me_space, there))

        def top_copy_two(i):
            there = lax.rem(me_space + 1 + i, m)
            return copy_to(top_mid.at[step], top_two.at[step, me_space], top_sems.at[step, 2, i],
                           top_sems.at[step, 3, me_space], (there, me))

        def start_one(i, carry):
            top_copy_one(i).start()
            return carry

        lax.fori_loop(0, n - 1, start_one, 0)
        for f in range(fluids):
            for side, (far, near) in enumerate(((bottom - 2, bottom - 1), (TOP + 1, TOP))):
                halo_send[step, side, f:f + 1, :] = rho[f, far:far + 1, :]
                halo_send[step, side, fluids + f:fluids + f + 1, :] = rho[f, near:near + 1, :]
                halo_send[step, side, 2 * fluids + f:2 * fluids + f + 1, :] = azi[f, near:near + 1, :]
        halos = []
        for side, there in enumerate((lax.rem(me_space + 1, m), lax.rem(me_space + m - 1, m))):
            halos.append(copy_to(halo_send.at[step, side], halo_recv.at[step, side],
                                 halo_sems.at[step, 0, side], halo_sems.at[step, 1, side],
                                 (there, me)))
        for halo in halos:
            halo.start()

        def radial(f, carry):
            for r in range(groups):
                here = rho[f, TOP + 8 * r:TOP + 8 * r + 8, :]
                speed = rad[f, TOP + 8 * r:TOP + 8 * r + 8, :]
                back = jnp.where(lanes >= 1, pltpu.roll(here, 1, 1), 0.0)
                ahead = jnp.where(lanes < cells - 1, pltpu.roll(here, cells - 1, 1), 0.0)
                down = 3.0 * here - ahead
                down_next = jnp.where(lanes < cells - 1, pltpu.roll(down, cells - 1, 1), 0.0)
                face = speed + jnp.where(
                    lanes < cells - 1, pltpu.roll(speed, cells - 1, 1), 0.0)
                flux = face * jnp.where(face > 0.0, 3.0 * here - back, down_next)
                before = jnp.where(
                    lanes >= 1, pltpu.roll(flux, 1, 1), jnp.minimum(speed, 0.0) * down)
                div[f, 8 * r:8 * r + 8, :] = flux - before
            return carry

        lax.fori_loop(0, fluids, radial, 0)

        for r in range(groups):
            here = rho[gas_at, TOP + 8 * r:TOP + 8 * r + 8, :]
            up = jnp.where(lanes < cells - 1, pltpu.roll(here, cells - 1, 1), here)
            low = jnp.where(lanes >= 1, pltpu.roll(here, 1, 1), here)
            push[0, 8 * r:8 * r + 8, :] = (up - low) * (0.5 / here)

        def wait_one(i, best):
            there = lax.rem(me + 1 + i, n)
            copy_to(top_send.at[step], top_one.at[step, there], top_sems.at[step, 0, i],
                    top_sems.at[step, 1, there], (me_space, there)).wait_recv()
            return jnp.maximum(best, top_one[step, there])

        top = lax.fori_loop(0, n - 1, wait_one, top)
        top_mid[step] = top

        def start_two(i, carry):
            top_copy_two(i).start()
            return carry

        lax.fori_loop(0, m - 1, start_two, 0)

        for halo in halos:
            halo.wait_recv()
        for f in range(fluids):
            for side, (far, near) in enumerate(((TOP - 2, TOP - 1), (bottom + 1, bottom))):
                rho[f, far:far + 1, :] = halo_recv[step, side, f:f + 1, :]
                rho[f, near:near + 1, :] = halo_recv[step, side, fluids + f:fluids + f + 1, :]
                azi[f, near:near + 1, :] = halo_recv[
                    step, side, 2 * fluids + f:2 * fluids + f + 1, :]

        def azimuthal(f, carry):
            for r in range(groups):
                at = TOP + 8 * r
                here = rho[f, at:at + 8, :]
                back_two = rho[f, at - 2:at + 6, :]
                back = rho[f, at - 1:at + 7, :]
                ahead = rho[f, at + 1:at + 9, :]
                ahead_two = rho[f, at + 2:at + 10, :]
                speed = azi[f, at:at + 8, :]
                low = speed + azi[f, at - 1:at + 7, :]
                high = speed + azi[f, at + 1:at + 9, :]
                after = high * jnp.where(high > 0.0, 3.0 * here - back, 3.0 * ahead - ahead_two)
                before = low * jnp.where(low > 0.0, 3.0 * back - back_two, 3.0 * here - ahead)
                div[f, 8 * r:8 * r + 8, :] += after - before
            return carry

        lax.fori_loop(0, fluids, azimuthal, 0)
        for r in range(groups):
            at = TOP + 8 * r
            push[1, 8 * r:8 * r + 8, :] = (
                rho[gas_at, at + 1:at + 9, :] - rho[gas_at, at - 1:at + 7, :]
            ) * (0.5 / rho[gas_at, at:at + 8, :])

        def wait_two(i, best):
            there = lax.rem(me_space + 1 + i, m)
            copy_to(top_mid.at[step], top_two.at[step, there], top_sems.at[step, 2, i],
                    top_sems.at[step, 3, there], (there, me)).wait_recv()
            return jnp.maximum(best, top_two[step, there])

        top = lax.fori_loop(0, m - 1, wait_two, top)
        fastest = jnp.max(jnp.max(top, axis=0, keepdims=True), axis=1, keepdims=True)
        dt = courant / (sound_speed + fastest)
        dt_quarter = 0.25 * dt

        def place(chunk):
            r = chunk // spans
            g = lax.rem(chunk, spans)
            cols = pl.ds(pl.multiple_of(width * g, 128), width)
            return (pl.ds(pl.multiple_of(TOP + 8 * r, 8), 8),
                    pl.ds(pl.multiple_of(8 * r, 8), 8), cols)

        def drag(chunk):
            rows, inner, cols = place(chunk)
            new_gas = rho[gas_at, rows, cols] - dt_quarter * div[gas_at, inner, cols]
            rho[gas_at, rows, cols] = new_gas
            sums = [jnp.zeros((8, width), jnp.float32)] * 3
            for k in range(local_species):
                scale = dt * inv_stop[k]
                new = rho[k, rows, cols] - dt_quarter * div[k, inner, cols]
                rho[k, rows, cols] = new
                factor = 1.0 / (1.0 + scale * new_gas)
                damp[k, inner, cols] = factor
                weight = (new * factor) * (scale * (1.0 / total_species))
                sums[0] = sums[0] + weight
                sums[1] = sums[1] + weight * rad[k, rows, cols]
                sums[2] = sums[2] + weight * azi[k, rows, cols]
            return sums

        def sib_copy(i):
            return copy_to(terms.at[step, 1 - core, i], sib_recv.at[step, i],
                           sib_sems.at[step, 0, i], sib_sems.at[step, 1, i], (me_space, sibling))

        def rs_copy(z):
            return copy_to(terms.at[step, core, z], rs_recv.at[step, chip],
                           rs_sems.at[step, 0, z], rs_sems.at[step, 1, chip],
                           (me_space, 2 * z + core))

        def rs_arrival(z):
            return copy_to(terms.at[step, core, z], rs_recv.at[step, z],
                           rs_sems.at[step, 0, z], rs_sems.at[step, 1, z],
                           (me_space, 2 * z + core))

        def farther(i):
            return lax.rem(chip + 1 + lax.rem(chips // 2 - 1 + i, chips - 1), chips)

        def for_sibling(z):
            sums = drag(2 * z + 1 - core)
            for part in range(3):
                terms[step, 1 - core, z, part] = sums[part]
            sib_copy(z).start()

        def for_sibling_step(i, carry):
            for_sibling(farther(i))
            return carry

        lax.fori_loop(0, chips - 1, for_sibling_step, 0)
        for_sibling(chip)

        def for_peers(i, carry):
            z = farther(i)
            sums = drag(2 * z + core)
            sib_copy(z).wait_recv()
            for part in range(3):
                terms[step, core, z, part] = sums[part] + sib_recv[step, z, part]
            rs_copy(z).start()
            return carry

        lax.fori_loop(0, chips - 1, for_peers, 0)
        sums = drag(me)
        sib_copy(chip).wait_recv()
        sums = tuple(sums[part] + sib_recv[step, chip, part] for part in range(3))

        def gather_sums(i, sums):
            z = lax.rem(chip + 1 + i, chips)
            rs_arrival(z).wait_recv()
            return tuple(sums[part] + rs_recv[step, z, part] for part in range(3))

        sums = lax.fori_loop(0, chips - 1, gather_sums, sums)

        rows, inner, cols = place(me)
        inverse = 1.0 / (1.0 + sums[0])
        gnew[step, me, 0] = (rad[gas_at, rows, cols] - dt * push[0, inner, cols] + sums[1]) * inverse
        gnew[step, me, 1] = (azi[gas_at, rows, cols] - dt * push[1, inner, cols] + sums[2]) * inverse

        def ag_copy(z):
            return copy_to(gnew.at[step, me], gnew.at[step, me], ag_sems.at[step, 0, z],
                           ag_sems.at[step, 1, chip], (me_space, 2 * z + core))

        def ag_arrival(z):
            return copy_to(gnew.at[step, 2 * z + core], gnew.at[step, 2 * z + core],
                           ag_sems.at[step, 0, z], ag_sems.at[step, 1, z],
                           (me_space, 2 * z + core))

        def fw_copy(z):
            return copy_to(gnew.at[step, 2 * z + core], gnew.at[step, 2 * z + core],
                           fw_sems.at[step, 0, z], fw_sems.at[step, 1, z], (me_space, sibling))

        def fw_arrival(z):
            other = 2 * z + 1 - core
            return copy_to(gnew.at[step, other], gnew.at[step, other],
                           fw_sems.at[step, 0, z], fw_sems.at[step, 1, z], (me_space, sibling))

        def start_ag(i, carry):
            ag_copy(farther(i)).start()
            return carry

        lax.fori_loop(0, chips - 1, start_ag, 0)
        fw_copy(chip).start()

        def update(chunk, best):
            rows, inner, cols = place(chunk)
            gas_rad = gnew[step, chunk, 0]
            gas_azi = gnew[step, chunk, 1]
            rad[gas_at, rows, cols] = gas_rad
            azi[gas_at, rows, cols] = gas_azi
            if step == STEPS - 1:
                return best
            speed = jnp.abs(gas_rad) + jnp.abs(gas_azi)
            for k in range(local_species):
                factor = damp[k, inner, cols]
                new_rad = gas_rad + (rad[k, rows, cols] - gas_rad) * factor
                new_azi = gas_azi + (azi[k, rows, cols] - gas_azi) * factor
                rad[k, rows, cols] = new_rad
                azi[k, rows, cols] = new_azi
                speed = jnp.maximum(speed, jnp.abs(new_rad) + jnp.abs(new_azi))
            return jnp.maximum(best, fold(speed))

        top = update(me, jnp.zeros((8, 128), jnp.float32))

        def update_peer(i, best):
            z = lax.rem(chip + 1 + i, chips)
            ag_arrival(z).wait_recv()
            fw_copy(z).start()
            return update(2 * z + core, best)

        top = lax.fori_loop(0, chips - 1, update_peer, top)

        def update_sibling(i, best):
            z = lax.rem(chip + i, chips)
            fw_arrival(z).wait_recv()
            return update(2 * z + 1 - core, best)

        top = lax.fori_loop(0, chips, update_sibling, top)

        unsent.append((top_copy_one, top_copy_two, sib_copy, rs_copy, ag_copy, fw_copy, halos))
        return top

    for step in range(STEPS):
        top = run_step(step, top)

    for top_copy_one, top_copy_two, sib_copy, rs_copy, ag_copy, fw_copy, halos in unsent:

        def sent_one(i, carry):
            top_copy_one(i).wait_send()
            return carry

        def sent_two(i, carry):
            top_copy_two(i).wait_send()
            return carry

        def sent_core(i, carry):
            sib_copy(i).wait_send()
            fw_copy(i).wait_send()
            return carry

        def sent_chip(i, carry):
            z = lax.rem(chip + 1 + i, chips)
            rs_copy(z).wait_send()
            ag_copy(z).wait_send()
            return carry

        lax.fori_loop(0, n - 1, sent_one, 0)
        lax.fori_loop(0, m - 1, sent_two, 0)
        lax.fori_loop(0, chips, sent_core, 0)
        lax.fori_loop(0, chips - 1, sent_chip, 0)
        for halo in halos:
            halo.wait_send()


def finish(rho, rad, azi, damp, dust_out, gas_out, new, sems):
    local_species, tile_rows, _ = damp.shape
    interior = pl.ds(TOP, tile_rows)
    copies = [pltpu.make_async_copy(
        rho.at[pl.ds(0, local_species), interior], dust_out.at[0], sems.at[0])]
    for part, held in enumerate((rho, rad, azi)):
        copies.append(pltpu.make_async_copy(
            held.at[local_species, interior], gas_out.at[part], sems.at[1 + part]))
    for copy in copies:
        copy.start()
    for k in range(local_species):
        for r in range(tile_rows // 8):
            rows = slice(TOP + 8 * r, TOP + 8 * r + 8)
            inner = slice(8 * r, 8 * r + 8)
            factor = damp[k, inner, :]
            for part, held in enumerate((rad, azi)):
                gas = held[local_species, rows, :]
                new[part, k, inner, :] = gas + (held[k, rows, :] - gas) * factor
        for part in range(2):
            copy = pltpu.make_async_copy(
                new.at[part, k], dust_out.at[part + 1, k], sems.at[4 + 2 * k + part])
            copy.start()
            copies.append(copy)
    for copy in copies:
        copy.wait()


def solution(mesh):
    n = mesh.shape["species"]
    m = mesh.shape["space"]

    def local(dust_state, gas_state, species_bin):
        local_species, tile_rows, cells = dust_state.shape[1:]
        fluids = local_species + 1
        groups = tile_rows // 8
        width = cells // (n // groups)
        chips = n // 2
        f32 = jnp.float32
        halo_rows = -(-3 * fluids // 8) * 8
        extended = pltpu.VMEM((fluids, tile_rows + 16, cells), f32)
        damped = pltpu.VMEM((local_species, tile_rows, cells), f32)
        dma = pltpu.SemaphoreType.DMA
        near = pl.BlockSpec(memory_space=pltpu.VMEM)
        far = pl.BlockSpec(memory_space=pltpu.HBM)
        held = pl.pallas_call(
            functools.partial(kernel, n, m),
            out_shape=(extended, extended, extended, damped),
            in_specs=[far, far, far],
            out_specs=(near,) * 4,
            scratch_shapes=[
                pltpu.SMEM((local_species,), jnp.int32),
                pltpu.VMEM((fluids, tile_rows, cells), f32),
                pltpu.VMEM((2, tile_rows, cells), f32),
                pltpu.VMEM((STEPS, 2, chips, 3, 8, width), f32),
                pltpu.VMEM((STEPS, n, 2, 8, width), f32),
                pltpu.VMEM((STEPS, chips, 3, 8, width), f32),
                pltpu.VMEM((STEPS, chips, 3, 8, width), f32),
                pltpu.VMEM((STEPS, 8, 128), f32),
                pltpu.VMEM((STEPS, n, 8, 128), f32),
                pltpu.VMEM((STEPS, 8, 128), f32),
                pltpu.VMEM((STEPS, m, 8, 128), f32),
                pltpu.VMEM((STEPS, 2, halo_rows, cells), f32),
                pltpu.VMEM((STEPS, 2, halo_rows, cells), f32),
                dma((7,)),
                dma((STEPS, 4, max(n, m))),
                dma((STEPS, 2, 2)),
                dma((STEPS, 2, chips)),
                dma((STEPS, 2, chips)),
                dma((STEPS, 2, chips)),
                dma((STEPS, 2, chips)),
            ],
            compiler_params=pltpu.CompilerParams(
                collective_id=0, has_side_effects=True, vmem_limit_bytes=58 * 1024 * 1024),
            cost_estimate=pl.CostEstimate(
                flops=200 * fluids * tile_rows * cells,
                bytes_accessed=24 * fluids * tile_rows * cells, transcendentals=0),
            name="disk_steps",
        )(dust_state, gas_state, species_bin)
        return pl.pallas_call(
            finish,
            out_shape=(jax.ShapeDtypeStruct(dust_state.shape, f32),
                       jax.ShapeDtypeStruct(gas_state.shape, f32)),
            in_specs=[near] * 4,
            out_specs=(far, far),
            scratch_shapes=[
                pltpu.VMEM((2, local_species, tile_rows, cells), f32),
                dma((4 + 2 * local_species,)),
            ],
            compiler_params=pltpu.CompilerParams(vmem_limit_bytes=20 * 1024 * 1024),
            name="last_update",
        )(*held)

    return jax.shard_map(
        local,
        mesh=mesh,
        in_specs=(P(None, "species", "space", None), P(None, "space", None), P("species")),
        out_specs=(P(None, "species", "space", None), P(None, "space", None)),
        check_vma=False,
    )
```

```python
import functools

import jax
import jax.numpy as jnp
from jax import lax
from jax.experimental import pallas as pl
from jax.experimental.pallas import tpu as pltpu
from jax.sharding import PartitionSpec as P

STEPS = 2

courant = 0.25
sound_speed = 1.0
stop_floor = 0.003
stop_span = 6.907755

MESH = pl.DeviceIdType.MESH
TOP = 8
HALVES = 2


def kernel(
    n, m, dust, gas, species_bins, rho, rad, azi, damp,
    species_bin, div, push, terms, gnew,
    sib_recv, rs_recv, top_send, top_one, top_mid, top_two, rho_send, rho_recv, azi_send, azi_recv,
    io_sem, top_sems, halo_sems, sib_sems, rs_sems, ag_sems, fw_sems,
):
    local_species, tile_rows, cells = dust.shape[1:]
    fluids = local_species + 1
    gas_at = local_species
    groups = tile_rows // 8
    spans = n // groups
    width = cells // spans
    halves = min(HALVES, width // 128)
    span = width // halves
    chips = n // 2
    total_species = local_species * n
    bottom = TOP + tile_rows

    me_space = lax.axis_index("space")
    me = lax.axis_index("species")
    core = lax.rem(me, 2)
    chip = me // 2
    sibling = me + 1 - 2 * core
    interior = pl.ds(TOP, tile_rows)

    barrier = pltpu.get_barrier_semaphore()

    def greet_species(i, carry):
        pl.semaphore_signal(
            barrier, inc=1, device_id=(me_space, lax.rem(me + 1 + i, n)), device_id_type=MESH)
        return carry

    def greet_space(i, carry):
        pl.semaphore_signal(
            barrier, inc=1, device_id=(lax.rem(me_space + 1 + i, m), me), device_id_type=MESH)
        return carry

    lax.fori_loop(0, n - 1, greet_species, 0)
    lax.fori_loop(0, m - 1, greet_space, 0)
    loads = []
    for part, held in enumerate((rho, rad, azi)):
        loads.append(pltpu.make_async_copy(
            dust.at[part], held.at[pl.ds(0, local_species), interior], io_sem.at[2 * part]))
        loads.append(pltpu.make_async_copy(
            gas.at[part], held.at[gas_at, interior], io_sem.at[2 * part + 1]))
    loads.append(pltpu.make_async_copy(species_bins, species_bin, io_sem.at[6]))
    for load in loads:
        load.start()
    for load in loads:
        load.wait()

    def fold(values):
        best = values[:, :128]
        for start in range(128, values.shape[1], 128):
            best = jnp.maximum(best, values[:, start:start + 128])
        return best

    def first_top(i, best):
        f = i // groups
        rows = pl.ds(pl.multiple_of(TOP + 8 * lax.rem(i, groups), 8), 8)
        return jnp.maximum(best, fold(jnp.abs(rad[f, rows, :]) + jnp.abs(azi[f, rows, :])))

    top = lax.fori_loop(0, fluids * groups, first_top, jnp.zeros((8, 128), jnp.float32))

    def copy_to(src, dst, send, recv, where):
        return pltpu.make_async_remote_copy(
            src_ref=src, dst_ref=dst, send_sem=send, recv_sem=recv,
            device_id=where, device_id_type=MESH)

    inv_stop = [
        jnp.exp(jnp.full((1, 1), species_bin[k].astype(jnp.float32))
                * (-stop_span / (total_species - 1))) * (1.0 / stop_floor)
        for k in range(local_species)]
    lanes = lax.broadcasted_iota(jnp.int32, (8, cells), 1)

    neighbours = (lax.rem(me_space + 1, m), lax.rem(me_space + m - 1, m))
    edges = ((bottom - 2, bottom - 1), (TOP + 1, TOP))
    beyond = ((TOP - 2, TOP - 1), (bottom + 1, bottom))

    def rho_halos(step):
        return [copy_to(rho_send.at[step, side], rho_recv.at[step, side],
                        halo_sems.at[step, 0, side], halo_sems.at[step, 1, side], (there, me))
                for side, there in enumerate(neighbours)]

    def azi_halos(step):
        return [copy_to(azi_send.at[step, side], azi_recv.at[step, side],
                        halo_sems.at[step, 2, side], halo_sems.at[step, 3, side], (there, me))
                for side, there in enumerate(neighbours)]

    def send_rho(step):
        for side, (far, near) in enumerate(edges):
            for f in range(fluids):
                rho_send[step, side, f:f + 1, :] = rho[f, far:far + 1, :]
                rho_send[step, side, fluids + f:fluids + f + 1, :] = rho[f, near:near + 1, :]
        for halo in rho_halos(step):
            halo.start()

    def send_azi(step):
        for side, (_, near) in enumerate(edges):
            for f in range(fluids):
                azi_send[step, side, f:f + 1, :] = azi[f, near:near + 1, :]
        for halo in azi_halos(step):
            halo.start()

    unsent = []

    def run_step(step, top):
        top_send[step] = top
        if step == 0:
            pl.semaphore_wait(barrier, n + m - 2)

        def top_copy_one(i):
            there = lax.rem(me_space + 1 + i, m)
            return copy_to(top_send.at[step], top_one.at[step, me_space], top_sems.at[step, 0, i],
                           top_sems.at[step, 1, me_space], (there, me))

        def top_copy_two(i):
            there = lax.rem(me + 1 + i, n)
            return copy_to(top_mid.at[step], top_two.at[step, me], top_sems.at[step, 2, i],
                           top_sems.at[step, 3, me], (me_space, there))

        def start_one(i, carry):
            top_copy_one(i).start()
            return carry

        lax.fori_loop(0, m - 1, start_one, 0)
        send_azi(step)
        if step == 0:
            send_rho(step)

        def radial(f, carry):
            for r in range(groups):
                here = rho[f, TOP + 8 * r:TOP + 8 * r + 8, :]
                speed = rad[f, TOP + 8 * r:TOP + 8 * r + 8, :]
                back = jnp.where(lanes >= 1, pltpu.roll(here, 1, 1), 0.0)
                ahead = jnp.where(lanes < cells - 1, pltpu.roll(here, cells - 1, 1), 0.0)
                down = 3.0 * here - ahead
                down_next = jnp.where(lanes < cells - 1, pltpu.roll(down, cells - 1, 1), 0.0)
                face = speed + jnp.where(
                    lanes < cells - 1, pltpu.roll(speed, cells - 1, 1), 0.0)
                flux = face * jnp.where(face > 0.0, 3.0 * here - back, down_next)
                before = jnp.where(
                    lanes >= 1, pltpu.roll(flux, 1, 1), jnp.minimum(speed, 0.0) * down)
                div[f, 8 * r:8 * r + 8, :] = flux - before
            return carry

        lax.fori_loop(0, fluids, radial, 0)

        for r in range(groups):
            here = rho[gas_at, TOP + 8 * r:TOP + 8 * r + 8, :]
            up = jnp.where(lanes < cells - 1, pltpu.roll(here, cells - 1, 1), here)
            low = jnp.where(lanes >= 1, pltpu.roll(here, 1, 1), here)
            push[0, 8 * r:8 * r + 8, :] = (up - low) * (0.5 / here)

        def wait_one(i, best):
            there = lax.rem(me_space + 1 + i, m)
            copy_to(top_send.at[step], top_one.at[step, there], top_sems.at[step, 0, i],
                    top_sems.at[step, 1, there], (there, me)).wait_recv()
            return jnp.maximum(best, top_one[step, there])

        top = lax.fori_loop(0, m - 1, wait_one, top)
        top_mid[step] = top

        def start_two(i, carry):
            top_copy_two(i).start()
            return carry

        lax.fori_loop(0, n - 1, start_two, 0)

        for halo in azi_halos(step) + rho_halos(step):
            halo.wait_recv()
        for side, (far, near) in enumerate(beyond):
            for f in range(fluids):
                rho[f, far:far + 1, :] = rho_recv[step, side, f:f + 1, :]
                rho[f, near:near + 1, :] = rho_recv[step, side, fluids + f:fluids + f + 1, :]
                azi[f, near:near + 1, :] = azi_recv[step, side, f:f + 1, :]

        def azimuthal(f, carry):
            for r in range(groups):
                at = TOP + 8 * r
                here = rho[f, at:at + 8, :]
                back_two = rho[f, at - 2:at + 6, :]
                back = rho[f, at - 1:at + 7, :]
                ahead = rho[f, at + 1:at + 9, :]
                ahead_two = rho[f, at + 2:at + 10, :]
                speed = azi[f, at:at + 8, :]
                low = speed + azi[f, at - 1:at + 7, :]
                high = speed + azi[f, at + 1:at + 9, :]
                after = high * jnp.where(high > 0.0, 3.0 * here - back, 3.0 * ahead - ahead_two)
                before = low * jnp.where(low > 0.0, 3.0 * back - back_two, 3.0 * here - ahead)
                div[f, 8 * r:8 * r + 8, :] += after - before
            return carry

        lax.fori_loop(0, fluids, azimuthal, 0)
        for r in range(groups):
            at = TOP + 8 * r
            push[1, 8 * r:8 * r + 8, :] = (
                rho[gas_at, at + 1:at + 9, :] - rho[gas_at, at - 1:at + 7, :]
            ) * (0.5 / rho[gas_at, at:at + 8, :])

        def wait_two(i, best):
            there = lax.rem(me + 1 + i, n)
            copy_to(top_mid.at[step], top_two.at[step, there], top_sems.at[step, 2, i],
                    top_sems.at[step, 3, there], (me_space, there)).wait_recv()
            return jnp.maximum(best, top_two[step, there])

        top = lax.fori_loop(0, n - 1, wait_two, top)
        fastest = jnp.max(jnp.max(top, axis=0, keepdims=True), axis=1, keepdims=True)
        dt = courant / (sound_speed + fastest)
        dt_quarter = 0.25 * dt

        def place(chunk, h):
            r = chunk // spans
            start = width * lax.rem(chunk, spans) + span * h
            return (pl.ds(pl.multiple_of(TOP + 8 * r, 8), 8),
                    pl.ds(pl.multiple_of(8 * r, 8), 8),
                    pl.ds(pl.multiple_of(start, 128), span))

        def drag(chunk, h):
            rows, inner, cols = place(chunk, h)
            new_gas = rho[gas_at, rows, cols] - dt_quarter * div[gas_at, inner, cols]
            rho[gas_at, rows, cols] = new_gas
            sums = [jnp.zeros((8, span), jnp.float32)] * 3
            for k in range(local_species):
                scale = dt * inv_stop[k]
                new = rho[k, rows, cols] - dt_quarter * div[k, inner, cols]
                rho[k, rows, cols] = new
                factor = 1.0 / (1.0 + scale * new_gas)
                damp[k, inner, cols] = factor
                weight = (new * factor) * (scale * (1.0 / total_species))
                sums[0] = sums[0] + weight
                sums[1] = sums[1] + weight * rad[k, rows, cols]
                sums[2] = sums[2] + weight * azi[k, rows, cols]
            return sums

        def farther(i):
            return lax.rem(chip + 1 + lax.rem(chips // 2 - 1 + i, chips - 1), chips)

        def sib_copy(z, h):
            return copy_to(terms.at[step, 1 - core, z, h], sib_recv.at[step, z, h],
                           sib_sems.at[step, 0, z, h], sib_sems.at[step, 1, z, h],
                           (me_space, sibling))

        def rs_copy(z, h):
            return copy_to(terms.at[step, core, z, h], rs_recv.at[step, chip, h],
                           rs_sems.at[step, 0, z, h], rs_sems.at[step, 1, chip, h],
                           (me_space, 2 * z + core))

        def rs_arrival(z, h):
            return copy_to(terms.at[step, core, z, h], rs_recv.at[step, z, h],
                           rs_sems.at[step, 0, z, h], rs_sems.at[step, 1, z, h],
                           (me_space, 2 * z + core))

        def ag_copy(z, h):
            return copy_to(gnew.at[step, me, h], gnew.at[step, me, h], ag_sems.at[step, 0, z, h],
                           ag_sems.at[step, 1, chip, h], (me_space, 2 * z + core))

        def ag_arrival(z, h):
            there = 2 * z + core
            return copy_to(gnew.at[step, there, h], gnew.at[step, there, h],
                           ag_sems.at[step, 0, z, h], ag_sems.at[step, 1, z, h],
                           (me_space, there))

        def fw_copy(z, h):
            there = 2 * z + core
            return copy_to(gnew.at[step, there, h], gnew.at[step, there, h],
                           fw_sems.at[step, 0, z, h], fw_sems.at[step, 1, z, h],
                           (me_space, sibling))

        def fw_arrival(z, h):
            there = 2 * z + 1 - core
            return copy_to(gnew.at[step, there, h], gnew.at[step, there, h],
                           fw_sems.at[step, 0, z, h], fw_sems.at[step, 1, z, h],
                           (me_space, sibling))

        own = []
        for h in range(halves):
            def for_sibling(z):
                sums = drag(2 * z + 1 - core, h)
                for part in range(3):
                    terms[step, 1 - core, z, h, part] = sums[part]
                sib_copy(z, h).start()

            def for_sibling_step(i, carry):
                for_sibling(farther(i))
                return carry

            lax.fori_loop(0, chips - 1, for_sibling_step, 0)
            for_sibling(chip)

            def for_peers(i, carry):
                z = farther(i)
                sums = drag(2 * z + core, h)
                sib_copy(z, h).wait_recv()
                for part in range(3):
                    terms[step, core, z, h, part] = sums[part] + sib_recv[step, z, h, part]
                rs_copy(z, h).start()
                return carry

            lax.fori_loop(0, chips - 1, for_peers, 0)
            own.append(drag(me, h))

        if step + 1 < STEPS:
            send_rho(step + 1)

        for h in range(halves):
            sib_copy(chip, h).wait_recv()

            def gather_sums(i, sums):
                z = lax.rem(chip + 1 + i, chips)
                rs_arrival(z, h).wait_recv()
                return tuple(sums[part] + rs_recv[step, z, h, part] for part in range(3))

            sums = lax.fori_loop(
                0, chips - 1, gather_sums,
                tuple(own[h][part] + sib_recv[step, chip, h, part] for part in range(3)))
            rows, inner, cols = place(me, h)
            inverse = 1.0 / (1.0 + sums[0])
            gnew[step, me, h, 0] = (
                rad[gas_at, rows, cols] - dt * push[0, inner, cols] + sums[1]) * inverse
            gnew[step, me, h, 1] = (
                azi[gas_at, rows, cols] - dt * push[1, inner, cols] + sums[2]) * inverse

            def start_ag(i, carry):
                ag_copy(farther(i), h).start()
                return carry

            lax.fori_loop(0, chips - 1, start_ag, 0)
            fw_copy(chip, h).start()

        def update(chunk, h, best):
            rows, inner, cols = place(chunk, h)
            gas_rad = gnew[step, chunk, h, 0]
            gas_azi = gnew[step, chunk, h, 1]
            rad[gas_at, rows, cols] = gas_rad
            azi[gas_at, rows, cols] = gas_azi
            if step == STEPS - 1:
                return best
            speed = jnp.abs(gas_rad) + jnp.abs(gas_azi)
            for k in range(local_species):
                factor = damp[k, inner, cols]
                new_rad = gas_rad + (rad[k, rows, cols] - gas_rad) * factor
                new_azi = gas_azi + (azi[k, rows, cols] - gas_azi) * factor
                rad[k, rows, cols] = new_rad
                azi[k, rows, cols] = new_azi
                speed = jnp.maximum(speed, jnp.abs(new_rad) + jnp.abs(new_azi))
            return jnp.maximum(best, fold(speed))

        top = jnp.zeros((8, 128), jnp.float32)
        for h in range(halves):
            top = update(me, h, top)

            def update_peer(i, best):
                z = lax.rem(chip + 1 + i, chips)
                ag_arrival(z, h).wait_recv()
                fw_copy(z, h).start()
                return update(2 * z + core, h, best)

            top = lax.fori_loop(0, chips - 1, update_peer, top)

            def update_sibling(i, best):
                z = lax.rem(chip + i, chips)
                fw_arrival(z, h).wait_recv()
                return update(2 * z + 1 - core, h, best)

            top = lax.fori_loop(0, chips, update_sibling, top)

        unsent.append((top_copy_one, top_copy_two, sib_copy, rs_copy, ag_copy, fw_copy,
                       rho_halos(step) + azi_halos(step)))
        return top

    for step in range(STEPS):
        top = run_step(step, top)

    for top_copy_one, top_copy_two, sib_copy, rs_copy, ag_copy, fw_copy, halos in unsent:

        def sent_one(i, carry):
            top_copy_one(i).wait_send()
            return carry

        def sent_two(i, carry):
            top_copy_two(i).wait_send()
            return carry

        def sent_core(i, carry):
            for h in range(halves):
                sib_copy(i, h).wait_send()
                fw_copy(i, h).wait_send()
            return carry

        def sent_chip(i, carry):
            z = lax.rem(chip + 1 + i, chips)
            for h in range(halves):
                rs_copy(z, h).wait_send()
                ag_copy(z, h).wait_send()
            return carry

        lax.fori_loop(0, m - 1, sent_one, 0)
        lax.fori_loop(0, n - 1, sent_two, 0)
        lax.fori_loop(0, chips, sent_core, 0)
        lax.fori_loop(0, chips - 1, sent_chip, 0)
        for halo in halos:
            halo.wait_send()


def finish(rho, rad, azi, damp, dust_out, gas_out, new, sems):
    local_species, tile_rows, _ = damp.shape
    interior = pl.ds(TOP, tile_rows)
    copies = [pltpu.make_async_copy(
        rho.at[pl.ds(0, local_species), interior], dust_out.at[0], sems.at[0])]
    for part, held in enumerate((rho, rad, azi)):
        copies.append(pltpu.make_async_copy(
            held.at[local_species, interior], gas_out.at[part], sems.at[1 + part]))
    for copy in copies:
        copy.start()
    for k in range(local_species):
        for r in range(tile_rows // 8):
            rows = slice(TOP + 8 * r, TOP + 8 * r + 8)
            inner = slice(8 * r, 8 * r + 8)
            factor = damp[k, inner, :]
            for part, held in enumerate((rad, azi)):
                gas = held[local_species, rows, :]
                new[part, k, inner, :] = gas + (held[k, rows, :] - gas) * factor
        for part in range(2):
            copy = pltpu.make_async_copy(
                new.at[part, k], dust_out.at[part + 1, k], sems.at[4 + 2 * k + part])
            copy.start()
            copies.append(copy)
    for copy in copies:
        copy.wait()


def solution(mesh):
    n = mesh.shape["species"]
    m = mesh.shape["space"]

    def local(dust_state, gas_state, species_bin):
        local_species, tile_rows, cells = dust_state.shape[1:]
        fluids = local_species + 1
        groups = tile_rows // 8
        width = cells // (n // groups)
        halves = min(HALVES, width // 128)
        span = width // halves
        chips = n // 2
        f32 = jnp.float32
        rho_rows = -(-2 * fluids // 8) * 8
        azi_rows = -(-fluids // 8) * 8
        extended = pltpu.VMEM((fluids, tile_rows + 16, cells), f32)
        damped = pltpu.VMEM((local_species, tile_rows, cells), f32)
        dma = pltpu.SemaphoreType.DMA
        near = pl.BlockSpec(memory_space=pltpu.VMEM)
        far = pl.BlockSpec(memory_space=pltpu.HBM)
        held = pl.pallas_call(
            functools.partial(kernel, n, m),
            out_shape=(extended, extended, extended, damped),
            in_specs=[far, far, far],
            out_specs=(near,) * 4,
            scratch_shapes=[
                pltpu.SMEM((local_species,), jnp.int32),
                pltpu.VMEM((fluids, tile_rows, cells), f32),
                pltpu.VMEM((2, tile_rows, cells), f32),
                pltpu.VMEM((STEPS, 2, chips, halves, 3, 8, span), f32),
                pltpu.VMEM((STEPS, n, halves, 2, 8, span), f32),
                pltpu.VMEM((STEPS, chips, halves, 3, 8, span), f32),
                pltpu.VMEM((STEPS, chips, halves, 3, 8, span), f32),
                pltpu.VMEM((STEPS, 8, 128), f32),
                pltpu.VMEM((STEPS, m, 8, 128), f32),
                pltpu.VMEM((STEPS, 8, 128), f32),
                pltpu.VMEM((STEPS, n, 8, 128), f32),
                pltpu.VMEM((STEPS, 2, rho_rows, cells), f32),
                pltpu.VMEM((STEPS, 2, rho_rows, cells), f32),
                pltpu.VMEM((STEPS, 2, azi_rows, cells), f32),
                pltpu.VMEM((STEPS, 2, azi_rows, cells), f32),
                dma((7,)),
                dma((STEPS, 4, max(n, m))),
                dma((STEPS, 4, 2)),
                dma((STEPS, 2, chips, halves)),
                dma((STEPS, 2, chips, halves)),
                dma((STEPS, 2, chips, halves)),
                dma((STEPS, 2, chips, halves)),
            ],
            compiler_params=pltpu.CompilerParams(
                collective_id=0, has_side_effects=True, vmem_limit_bytes=58 * 1024 * 1024),
            cost_estimate=pl.CostEstimate(
                flops=200 * fluids * tile_rows * cells,
                bytes_accessed=24 * fluids * tile_rows * cells, transcendentals=0),
            name="disk_steps",
        )(dust_state, gas_state, species_bin)
        return pl.pallas_call(
            finish,
            out_shape=(jax.ShapeDtypeStruct(dust_state.shape, f32),
                       jax.ShapeDtypeStruct(gas_state.shape, f32)),
            in_specs=[near] * 4,
            out_specs=(far, far),
            scratch_shapes=[
                pltpu.VMEM((2, local_species, tile_rows, cells), f32),
                dma((4 + 2 * local_species,)),
            ],
            compiler_params=pltpu.CompilerParams(vmem_limit_bytes=20 * 1024 * 1024),
            name="last_update",
        )(*held)

    return jax.shard_map(
        local,
        mesh=mesh,
        in_specs=(P(None, "species", "space", None), P(None, "space", None), P("species")),
        out_specs=(P(None, "species", "space", None), P(None, "space", None)),
        check_vma=False,
    )
```

```python
import functools

import jax
import jax.numpy as jnp
from jax import lax
from jax.experimental import pallas as pl
from jax.experimental.pallas import tpu as pltpu
from jax.sharding import PartitionSpec as P

STEPS = 2

courant = 0.25
sound_speed = 1.0
stop_floor = 0.003
stop_span = 6.907755

MESH = pl.DeviceIdType.MESH
TOP = 8
HALVES = 1


def loop(count, body, carry):
    if count > 8:
        return lax.fori_loop(0, count, body, carry)
    for i in range(count):
        carry = body(i, carry)
    return carry


def kernel(
    n, m, dust, gas, species_bins, rho, rad, azi, damp,
    species_bin, div, push, terms, gnew,
    sib_recv, rs_recv, top_send, top_one, top_mid, top_two, rho_send, rho_recv, azi_send, azi_recv,
    io_sem, top_sems, halo_sems, sib_sems, rs_sems, ag_sems, fw_sems,
):
    local_species, tile_rows, cells = dust.shape[1:]
    fluids = local_species + 1
    gas_at = local_species
    groups = tile_rows // 8
    spans = n // groups
    width = cells // spans
    halves = min(HALVES, width // 128)
    span = width // halves
    chips = n // 2
    total_species = local_species * n
    bottom = TOP + tile_rows

    me_space = lax.axis_index("space")
    me = lax.axis_index("species")
    core = lax.rem(me, 2)
    chip = me // 2
    sibling = me + 1 - 2 * core
    interior = pl.ds(TOP, tile_rows)

    barrier = pltpu.get_barrier_semaphore()

    def greet_species(i, carry):
        pl.semaphore_signal(
            barrier, inc=1, device_id=(me_space, lax.rem(me + 1 + i, n)), device_id_type=MESH)
        return carry

    def greet_space(i, carry):
        pl.semaphore_signal(
            barrier, inc=1, device_id=(lax.rem(me_space + 1 + i, m), me), device_id_type=MESH)
        return carry

    loop(n - 1, greet_species, 0)
    loop(m - 1, greet_space, 0)
    loads = []
    for part, held in enumerate((rho, rad, azi)):
        loads.append(pltpu.make_async_copy(
            dust.at[part], held.at[pl.ds(0, local_species), interior], io_sem.at[2 * part]))
        loads.append(pltpu.make_async_copy(
            gas.at[part], held.at[gas_at, interior], io_sem.at[2 * part + 1]))
    loads.append(pltpu.make_async_copy(species_bins, species_bin, io_sem.at[6]))
    for load in loads:
        load.start()
    for load in loads:
        load.wait()

    def fold(values):
        best = values[:, :128]
        for start in range(128, values.shape[1], 128):
            best = jnp.maximum(best, values[:, start:start + 128])
        return best

    def first_top(f, best):
        for at in range(TOP, bottom, 8):
            best = jnp.maximum(
                best, fold(jnp.abs(rad[f, at:at + 8, :]) + jnp.abs(azi[f, at:at + 8, :])))
        return best

    top = lax.fori_loop(0, fluids, first_top, jnp.zeros((8, 128), jnp.float32))

    def copy_to(src, dst, send, recv, where):
        return pltpu.make_async_remote_copy(
            src_ref=src, dst_ref=dst, send_sem=send, recv_sem=recv,
            device_id=where, device_id_type=MESH)

    inv_stop = [
        jnp.exp(jnp.full((1, 1), species_bin[k].astype(jnp.float32))
                * (-stop_span / (total_species - 1))) * (1.0 / stop_floor)
        for k in range(local_species)]
    lanes = lax.broadcasted_iota(jnp.int32, (8, cells), 1)

    neighbours = (lax.rem(me_space + 1, m), lax.rem(me_space + m - 1, m))
    edges = ((bottom - 2, bottom - 1), (TOP + 1, TOP))
    beyond = ((TOP - 2, TOP - 1), (bottom + 1, bottom))

    def rho_halos(step):
        return [copy_to(rho_send.at[step, side], rho_recv.at[step, side],
                        halo_sems.at[step, 0, side], halo_sems.at[step, 1, side], (there, me))
                for side, there in enumerate(neighbours)]

    def azi_halos(step):
        return [copy_to(azi_send.at[step, side], azi_recv.at[step, side],
                        halo_sems.at[step, 2, side], halo_sems.at[step, 3, side], (there, me))
                for side, there in enumerate(neighbours)]

    def send_rho(step):
        for side, (far, near) in enumerate(edges):
            for f in range(fluids):
                rho_send[step, side, f:f + 1, :] = rho[f, far:far + 1, :]
                rho_send[step, side, fluids + f:fluids + f + 1, :] = rho[f, near:near + 1, :]
        for halo in rho_halos(step):
            halo.start()

    def send_azi(step):
        for side, (_, near) in enumerate(edges):
            for f in range(fluids):
                azi_send[step, side, f:f + 1, :] = azi[f, near:near + 1, :]
        for halo in azi_halos(step):
            halo.start()

    unsent = []

    def run_step(step, top):
        top_send[step] = top
        if step == 0:
            pl.semaphore_wait(barrier, n + m - 2)

        def top_copy_one(i):
            there = lax.rem(me_space + 1 + i, m)
            return copy_to(top_send.at[step], top_one.at[step, i], top_sems.at[step, 0],
                           top_sems.at[step, 1], (there, me))

        def top_copy_two(i):
            there = lax.rem(me + 1 + i, n)
            return copy_to(top_mid.at[step], top_two.at[step, i], top_sems.at[step, 2],
                           top_sems.at[step, 3], (me_space, there))

        def top_all_one():
            return copy_to(top_one.at[step], top_one.at[step], top_sems.at[step, 0],
                           top_sems.at[step, 1], (neighbours[0], me))

        def top_all_two():
            return copy_to(top_two.at[step], top_two.at[step], top_sems.at[step, 2],
                           top_sems.at[step, 3], (me_space, sibling))

        def start_one(i, carry):
            top_copy_one(i).start()
            return carry

        loop(m - 1, start_one, 0)
        send_azi(step)
        if step == 0:
            send_rho(step)

        def radial(f, carry):
            for r in range(groups):
                here = rho[f, TOP + 8 * r:TOP + 8 * r + 8, :]
                speed = rad[f, TOP + 8 * r:TOP + 8 * r + 8, :]
                back = jnp.where(lanes >= 1, pltpu.roll(here, 1, 1), 0.0)
                ahead = jnp.where(lanes < cells - 1, pltpu.roll(here, cells - 1, 1), 0.0)
                down = 3.0 * here - ahead
                down_next = jnp.where(lanes < cells - 1, pltpu.roll(down, cells - 1, 1), 0.0)
                face = speed + jnp.where(
                    lanes < cells - 1, pltpu.roll(speed, cells - 1, 1), 0.0)
                flux = face * jnp.where(face > 0.0, 3.0 * here - back, down_next)
                before = jnp.where(
                    lanes >= 1, pltpu.roll(flux, 1, 1), jnp.minimum(speed, 0.0) * down)
                div[f, 8 * r:8 * r + 8, :] = flux - before
            return carry

        lax.fori_loop(0, fluids, radial, 0)

        for r in range(groups):
            here = rho[gas_at, TOP + 8 * r:TOP + 8 * r + 8, :]
            up = jnp.where(lanes < cells - 1, pltpu.roll(here, cells - 1, 1), here)
            low = jnp.where(lanes >= 1, pltpu.roll(here, 1, 1), here)
            push[0, 8 * r:8 * r + 8, :] = (up - low) * (0.5 / here)

        top_all_one().wait_recv()
        for i in range(m - 1):
            top = jnp.maximum(top, top_one[step, i])
        top_mid[step] = top

        def start_two(i, carry):
            top_copy_two(i).start()
            return carry

        loop(n - 1, start_two, 0)

        for halo in azi_halos(step) + rho_halos(step):
            halo.wait_recv()
        for side, (far, near) in enumerate(beyond):
            for f in range(fluids):
                rho[f, far:far + 1, :] = rho_recv[step, side, f:f + 1, :]
                rho[f, near:near + 1, :] = rho_recv[step, side, fluids + f:fluids + f + 1, :]
                azi[f, near:near + 1, :] = azi_recv[step, side, f:f + 1, :]

        def azimuthal(f, carry):
            for r in range(groups):
                at = TOP + 8 * r
                here = rho[f, at:at + 8, :]
                back_two = rho[f, at - 2:at + 6, :]
                back = rho[f, at - 1:at + 7, :]
                ahead = rho[f, at + 1:at + 9, :]
                ahead_two = rho[f, at + 2:at + 10, :]
                speed = azi[f, at:at + 8, :]
                low = speed + azi[f, at - 1:at + 7, :]
                high = speed + azi[f, at + 1:at + 9, :]
                after = high * jnp.where(high > 0.0, 3.0 * here - back, 3.0 * ahead - ahead_two)
                before = low * jnp.where(low > 0.0, 3.0 * back - back_two, 3.0 * here - ahead)
                div[f, 8 * r:8 * r + 8, :] += after - before
            return carry

        lax.fori_loop(0, fluids, azimuthal, 0)
        for r in range(groups):
            at = TOP + 8 * r
            push[1, 8 * r:8 * r + 8, :] = (
                rho[gas_at, at + 1:at + 9, :] - rho[gas_at, at - 1:at + 7, :]
            ) * (0.5 / rho[gas_at, at:at + 8, :])

        top_all_two().wait_recv()
        for i in range(n - 1):
            top = jnp.maximum(top, top_two[step, i])
        fastest = jnp.max(jnp.max(top, axis=0, keepdims=True), axis=1, keepdims=True)
        dt = courant / (sound_speed + fastest)
        dt_quarter = 0.25 * dt

        def place(chunk, h):
            r = chunk // spans
            start = width * lax.rem(chunk, spans) + span * h
            return (pl.ds(pl.multiple_of(TOP + 8 * r, 8), 8),
                    pl.ds(pl.multiple_of(8 * r, 8), 8),
                    pl.ds(pl.multiple_of(start, 128), span))

        def drag(chunk, h):
            rows, inner, cols = place(chunk, h)
            new_gas = rho[gas_at, rows, cols] - dt_quarter * div[gas_at, inner, cols]
            rho[gas_at, rows, cols] = new_gas
            sums = [jnp.zeros((8, span), jnp.float32)] * 3
            for k in range(local_species):
                scale = dt * inv_stop[k]
                new = rho[k, rows, cols] - dt_quarter * div[k, inner, cols]
                rho[k, rows, cols] = new
                factor = 1.0 / (1.0 + scale * new_gas)
                damp[k, inner, cols] = factor
                weight = (new * factor) * (scale * (1.0 / total_species))
                sums[0] = sums[0] + weight
                sums[1] = sums[1] + weight * rad[k, rows, cols]
                sums[2] = sums[2] + weight * azi[k, rows, cols]
            return sums

        def farther(i):
            return lax.rem(chip + 1 + (chips // 2 - 1 + i) % (chips - 1), chips)

        def sib_copy(z, h):
            return copy_to(terms.at[step, 1 - core, z, h], sib_recv.at[step, z, h],
                           sib_sems.at[step, 0, 0, 0], sib_sems.at[step, 1, z, h],
                           (me_space, sibling))

        def rs_copy(z, h):
            slot = lax.rem(z + chips - 1 - chip, chips)
            return copy_to(terms.at[step, core, z, h], rs_recv.at[step, h, slot],
                           rs_sems.at[step, 0, 0], rs_sems.at[step, 1, h],
                           (me_space, 2 * z + core))

        def rs_all(h):
            return copy_to(rs_recv.at[step, h], rs_recv.at[step, h], rs_sems.at[step, 0, 0],
                           rs_sems.at[step, 1, h], (me_space, sibling))

        def rs_sent():
            return copy_to(rs_recv.at[step], rs_recv.at[step], rs_sems.at[step, 0, 0],
                           rs_sems.at[step, 1, 0], (me_space, sibling))

        def sib_sent():
            held = terms.at[step, 1 - core]
            return copy_to(held, held, sib_sems.at[step, 0, 0, 0], sib_sems.at[step, 1, 0, 0],
                           (me_space, sibling))

        def ag_sent():
            held = gnew.at[step, pl.ds(0, chips - 1)]
            return copy_to(held, held, ag_sems.at[step, 0, 0, 0], ag_sems.at[step, 1, 0, 0],
                           (me_space, sibling))

        def fw_sent():
            held = gnew.at[step, pl.ds(0, chips)]
            return copy_to(held, held, fw_sems.at[step, 0, 0, 0], fw_sems.at[step, 1, 0, 0],
                           (me_space, sibling))

        def ag_copy(z, h):
            return copy_to(gnew.at[step, me, h], gnew.at[step, me, h], ag_sems.at[step, 0, 0, 0],
                           ag_sems.at[step, 1, chip, h], (me_space, 2 * z + core))

        def ag_arrival(z, h):
            there = 2 * z + core
            return copy_to(gnew.at[step, there, h], gnew.at[step, there, h],
                           ag_sems.at[step, 0, 0, 0], ag_sems.at[step, 1, z, h],
                           (me_space, there))

        def fw_copy(z, h):
            there = 2 * z + core
            return copy_to(gnew.at[step, there, h], gnew.at[step, there, h],
                           fw_sems.at[step, 0, 0, 0], fw_sems.at[step, 1, z, h],
                           (me_space, sibling))

        def fw_arrival(z, h):
            there = 2 * z + 1 - core
            return copy_to(gnew.at[step, there, h], gnew.at[step, there, h],
                           fw_sems.at[step, 0, 0, 0], fw_sems.at[step, 1, z, h],
                           (me_space, sibling))

        own = []
        for h in range(halves):
            def for_sibling(z):
                sums = drag(2 * z + 1 - core, h)
                for part in range(3):
                    terms[step, 1 - core, z, h, part] = sums[part]
                sib_copy(z, h).start()

            def for_sibling_step(i, carry):
                for_sibling(farther(i))
                return carry

            loop(chips - 1, for_sibling_step, 0)
            for_sibling(chip)

            def for_peers(i, carry):
                z = farther(i)
                sums = drag(2 * z + core, h)
                sib_copy(z, h).wait_recv()
                for part in range(3):
                    terms[step, core, z, h, part] = sums[part] + sib_recv[step, z, h, part]
                rs_copy(z, h).start()
                return carry

            loop(chips - 1, for_peers, 0)
            own.append(drag(me, h))

        if step + 1 < STEPS:
            send_rho(step + 1)

        for h in range(halves):
            sib_copy(chip, h).wait_recv()

            sums = [own[h][part] + sib_recv[step, chip, h, part] for part in range(3)]
            rs_all(h).wait_recv()
            for i in range(chips - 1):
                sums = [sums[part] + rs_recv[step, h, i, part] for part in range(3)]
            rows, inner, cols = place(me, h)
            inverse = 1.0 / (1.0 + sums[0])
            gnew[step, me, h, 0] = (
                rad[gas_at, rows, cols] - dt * push[0, inner, cols] + sums[1]) * inverse
            gnew[step, me, h, 1] = (
                azi[gas_at, rows, cols] - dt * push[1, inner, cols] + sums[2]) * inverse

            def start_ag(i, carry):
                ag_copy(farther(i), h).start()
                return carry

            loop(chips - 1, start_ag, 0)
            fw_copy(chip, h).start()

        def update(chunk, h, best):
            rows, inner, cols = place(chunk, h)
            gas_rad = gnew[step, chunk, h, 0]
            gas_azi = gnew[step, chunk, h, 1]
            rad[gas_at, rows, cols] = gas_rad
            azi[gas_at, rows, cols] = gas_azi
            if step == STEPS - 1:
                return best
            speed = jnp.abs(gas_rad) + jnp.abs(gas_azi)
            for k in range(local_species):
                factor = damp[k, inner, cols]
                new_rad = gas_rad + (rad[k, rows, cols] - gas_rad) * factor
                new_azi = gas_azi + (azi[k, rows, cols] - gas_azi) * factor
                rad[k, rows, cols] = new_rad
                azi[k, rows, cols] = new_azi
                speed = jnp.maximum(speed, jnp.abs(new_rad) + jnp.abs(new_azi))
            return jnp.maximum(best, fold(speed))

        top = jnp.zeros((8, 128), jnp.float32)
        for h in range(halves):
            top = update(me, h, top)

            def update_peer(i, best):
                z = lax.rem(chip + 1 + i, chips)
                ag_arrival(z, h).wait_recv()
                fw_copy(z, h).start()
                return update(2 * z + core, h, best)

            top = loop(chips - 1, update_peer, top)

            def update_sibling(i, best):
                z = lax.rem(chip + i, chips)
                fw_arrival(z, h).wait_recv()
                return update(2 * z + 1 - core, h, best)

            top = loop(chips, update_sibling, top)

        unsent.append((top_all_one(), top_all_two(), sib_sent(), rs_sent(), ag_sent(), fw_sent(),
                       *rho_halos(step), *azi_halos(step)))
        return top

    for step in range(STEPS):
        top = run_step(step, top)

    for sends in unsent:
        for send in sends:
            send.wait_send()


def finish(rho, rad, azi, damp, dust_out, gas_out, new, sems):
    local_species, tile_rows, _ = damp.shape
    interior = pl.ds(TOP, tile_rows)
    copies = [pltpu.make_async_copy(
        rho.at[pl.ds(0, local_species), interior], dust_out.at[0], sems.at[0])]
    for part, held in enumerate((rho, rad, azi)):
        copies.append(pltpu.make_async_copy(
            held.at[local_species, interior], gas_out.at[part], sems.at[1 + part]))
    for copy in copies:
        copy.start()
    for k in range(local_species):
        for r in range(tile_rows // 8):
            rows = slice(TOP + 8 * r, TOP + 8 * r + 8)
            inner = slice(8 * r, 8 * r + 8)
            factor = damp[k, inner, :]
            for part, held in enumerate((rad, azi)):
                gas = held[local_species, rows, :]
                new[part, k, inner, :] = gas + (held[k, rows, :] - gas) * factor
        for part in range(2):
            copy = pltpu.make_async_copy(
                new.at[part, k], dust_out.at[part + 1, k], sems.at[4 + 2 * k + part])
            copy.start()
            copies.append(copy)
    for copy in copies:
        copy.wait()


def solution(mesh):
    n = mesh.shape["species"]
    m = mesh.shape["space"]

    def local(dust_state, gas_state, species_bin):
        local_species, tile_rows, cells = dust_state.shape[1:]
        fluids = local_species + 1
        groups = tile_rows // 8
        width = cells // (n // groups)
        halves = min(HALVES, width // 128)
        span = width // halves
        chips = n // 2
        f32 = jnp.float32
        rho_rows = -(-2 * fluids // 8) * 8
        azi_rows = -(-fluids // 8) * 8
        extended = pltpu.VMEM((fluids, tile_rows + 16, cells), f32)
        damped = pltpu.VMEM((local_species, tile_rows, cells), f32)
        dma = pltpu.SemaphoreType.DMA
        near = pl.BlockSpec(memory_space=pltpu.VMEM)
        far = pl.BlockSpec(memory_space=pltpu.HBM)
        held = pl.pallas_call(
            functools.partial(kernel, n, m),
            out_shape=(extended, extended, extended, damped),
            in_specs=[far, far, far],
            out_specs=(near,) * 4,
            scratch_shapes=[
                pltpu.SMEM((local_species,), jnp.int32),
                pltpu.VMEM((fluids, tile_rows, cells), f32),
                pltpu.VMEM((2, tile_rows, cells), f32),
                pltpu.VMEM((STEPS, 2, chips, halves, 3, 8, span), f32),
                pltpu.VMEM((STEPS, n, halves, 2, 8, span), f32),
                pltpu.VMEM((STEPS, chips, halves, 3, 8, span), f32),
                pltpu.VMEM((STEPS, halves, chips - 1, 3, 8, span), f32),
                pltpu.VMEM((STEPS, 8, 128), f32),
                pltpu.VMEM((STEPS, m - 1, 8, 128), f32),
                pltpu.VMEM((STEPS, 8, 128), f32),
                pltpu.VMEM((STEPS, n - 1, 8, 128), f32),
                pltpu.VMEM((STEPS, 2, rho_rows, cells), f32),
                pltpu.VMEM((STEPS, 2, rho_rows, cells), f32),
                pltpu.VMEM((STEPS, 2, azi_rows, cells), f32),
                pltpu.VMEM((STEPS, 2, azi_rows, cells), f32),
                dma((7,)),
                dma((STEPS, 4)),
                dma((STEPS, 4, 2)),
                dma((STEPS, 2, chips, halves)),
                dma((STEPS, 2, halves)),
                dma((STEPS, 2, chips, halves)),
                dma((STEPS, 2, chips, halves)),
            ],
            compiler_params=pltpu.CompilerParams(
                collective_id=0, has_side_effects=True, vmem_limit_bytes=58 * 1024 * 1024),
            cost_estimate=pl.CostEstimate(
                flops=200 * fluids * tile_rows * cells,
                bytes_accessed=24 * fluids * tile_rows * cells, transcendentals=0),
            name="disk_steps",
        )(dust_state, gas_state, species_bin)
        return pl.pallas_call(
            finish,
            out_shape=(jax.ShapeDtypeStruct(dust_state.shape, f32),
                       jax.ShapeDtypeStruct(gas_state.shape, f32)),
            in_specs=[near] * 4,
            out_specs=(far, far),
            scratch_shapes=[
                pltpu.VMEM((2, local_species, tile_rows, cells), f32),
                dma((4 + 2 * local_species,)),
            ],
            compiler_params=pltpu.CompilerParams(vmem_limit_bytes=20 * 1024 * 1024),
            name="last_update",
        )(*held)

    return jax.shard_map(
        local,
        mesh=mesh,
        in_specs=(P(None, "species", "space", None), P(None, "space", None), P("species")),
        out_specs=(P(None, "species", "space", None), P(None, "space", None)),
        check_vma=False,
    )
```

```python
import functools

import jax
import jax.numpy as jnp
from jax import lax
from jax.experimental import pallas as pl
from jax.experimental.pallas import tpu as pltpu
from jax.sharding import PartitionSpec as P

STEPS = 2

courant = 0.25
sound_speed = 1.0
stop_floor = 0.003
stop_span = 6.907755

MESH = pl.DeviceIdType.MESH
TOP = 8
HALVES = 1


def loop(count, body, carry):
    if count > 8:
        return lax.fori_loop(0, count, body, carry)
    for i in range(count):
        carry = body(i, carry)
    return carry


def kernel(
    n, m, dust, gas, species_bins, rho, rad, azi, damp,
    species_bin, div, push, terms, gnew,
    sib_recv, rs_recv, top_send, top_one, top_mid, top_two, rho_send, rho_recv, azi_send, azi_recv,
    io_sem, top_sems, halo_sems, sib_sems, rs_sems, ag_sems, fw_sems,
):
    local_species, tile_rows, cells = dust.shape[1:]
    fluids = local_species + 1
    gas_at = local_species
    groups = tile_rows // 8
    spans = n // groups
    width = cells // spans
    halves = min(HALVES, width // 128)
    span = width // halves
    chips = n // 2
    total_species = local_species * n
    bottom = TOP + tile_rows

    me_space = lax.axis_index("space")
    me = lax.axis_index("species")
    core = lax.rem(me, 2)
    chip = me // 2
    sibling = me + 1 - 2 * core
    interior = pl.ds(TOP, tile_rows)

    barrier = pltpu.get_barrier_semaphore()

    def greet_species(i, carry):
        pl.semaphore_signal(
            barrier, inc=1, device_id=(me_space, lax.rem(me + 1 + i, n)), device_id_type=MESH)
        return carry

    def greet_space(i, carry):
        pl.semaphore_signal(
            barrier, inc=1, device_id=(lax.rem(me_space + 1 + i, m), me), device_id_type=MESH)
        return carry

    loop(n - 1, greet_species, 0)
    loop(m - 1, greet_space, 0)
    loads = []
    for part, held in enumerate((rho, rad, azi)):
        loads.append(pltpu.make_async_copy(
            dust.at[part], held.at[pl.ds(0, local_species), interior], io_sem.at[2 * part]))
        loads.append(pltpu.make_async_copy(
            gas.at[part], held.at[gas_at, interior], io_sem.at[2 * part + 1]))
    loads.append(pltpu.make_async_copy(species_bins, species_bin, io_sem.at[6]))
    for load in loads:
        load.start()
    for load in loads:
        load.wait()

    def fold(values):
        best = values[:, :128]
        for start in range(128, values.shape[1], 128):
            best = jnp.maximum(best, values[:, start:start + 128])
        return best

    def first_top(f, best):
        for at in range(TOP, bottom, 8):
            best = jnp.maximum(
                best, fold(jnp.abs(rad[f, at:at + 8, :]) + jnp.abs(azi[f, at:at + 8, :])))
        return best

    top = lax.fori_loop(0, fluids, first_top, jnp.zeros((8, 128), jnp.float32))

    def copy_to(src, dst, send, recv, where):
        return pltpu.make_async_remote_copy(
            src_ref=src, dst_ref=dst, send_sem=send, recv_sem=recv,
            device_id=where, device_id_type=MESH)

    inv_stop = [
        jnp.exp(jnp.full((1, 1), species_bin[k].astype(jnp.float32))
                * (-stop_span / (total_species - 1))) * (1.0 / stop_floor)
        for k in range(local_species)]
    lanes = lax.broadcasted_iota(jnp.int32, (8, cells), 1)

    neighbours = (lax.rem(me_space + 1, m), lax.rem(me_space + m - 1, m))
    edges = ((bottom - 2, bottom - 1), (TOP + 1, TOP))
    beyond = ((TOP - 2, TOP - 1), (bottom + 1, bottom))

    def rho_halos(step):
        return [copy_to(rho_send.at[step, side], rho_recv.at[step, side],
                        halo_sems.at[step, 0, side], halo_sems.at[step, 1, side], (there, me))
                for side, there in enumerate(neighbours)]

    def azi_halos(step):
        return [copy_to(azi_send.at[step, side], azi_recv.at[step, side],
                        halo_sems.at[step, 2, side], halo_sems.at[step, 3, side], (there, me))
                for side, there in enumerate(neighbours)]

    def send_rho(step):
        for side, (far, near) in enumerate(edges):
            for f in range(fluids):
                rho_send[step, side, f:f + 1, :] = rho[f, far:far + 1, :]
                rho_send[step, side, fluids + f:fluids + f + 1, :] = rho[f, near:near + 1, :]
        for halo in rho_halos(step):
            halo.start()

    def send_azi(step):
        for side, (_, near) in enumerate(edges):
            for f in range(fluids):
                azi_send[step, side, f:f + 1, :] = azi[f, near:near + 1, :]
        for halo in azi_halos(step):
            halo.start()

    unsent = []

    def run_step(step, top):
        top_send[step] = top
        if step == 0:
            pl.semaphore_wait(barrier, n + m - 2)

        def top_copy_one(i):
            there = lax.rem(me_space + 1 + i, m)
            return copy_to(top_send.at[step], top_one.at[step, i], top_sems.at[step, 0],
                           top_sems.at[step, 1], (there, me))

        def top_copy_two(i):
            there = lax.rem(me + 1 + i, n)
            return copy_to(top_mid.at[step], top_two.at[step, i], top_sems.at[step, 2],
                           top_sems.at[step, 3], (me_space, there))

        def top_all_one():
            return copy_to(top_one.at[step], top_one.at[step], top_sems.at[step, 0],
                           top_sems.at[step, 1], (neighbours[0], me))

        def top_all_two():
            return copy_to(top_two.at[step], top_two.at[step], top_sems.at[step, 2],
                           top_sems.at[step, 3], (me_space, sibling))

        def start_one(i, carry):
            top_copy_one(i).start()
            return carry

        loop(m - 1, start_one, 0)
        send_azi(step)
        if step == 0:
            send_rho(step)

        def radial(f, carry):
            for r in range(groups):
                here = rho[f, TOP + 8 * r:TOP + 8 * r + 8, :]
                speed = rad[f, TOP + 8 * r:TOP + 8 * r + 8, :]
                back = jnp.where(lanes >= 1, pltpu.roll(here, 1, 1), 0.0)
                ahead = jnp.where(lanes < cells - 1, pltpu.roll(here, cells - 1, 1), 0.0)
                down = 3.0 * here - ahead
                down_next = jnp.where(lanes < cells - 1, pltpu.roll(down, cells - 1, 1), 0.0)
                face = speed + jnp.where(
                    lanes < cells - 1, pltpu.roll(speed, cells - 1, 1), 0.0)
                flux = face * jnp.where(face > 0.0, 3.0 * here - back, down_next)
                before = jnp.where(
                    lanes >= 1, pltpu.roll(flux, 1, 1), jnp.minimum(speed, 0.0) * down)
                div[f, 8 * r:8 * r + 8, :] = flux - before
            return carry

        early = fluids * 2 // 5
        lax.fori_loop(0, early, radial, 0)

        top_all_one().wait_recv()
        for i in range(m - 1):
            top = jnp.maximum(top, top_one[step, i])
        top_mid[step] = top

        def start_two(i, carry):
            top_copy_two(i).start()
            return carry

        loop(n - 1, start_two, 0)

        lax.fori_loop(early, fluids, radial, 0)
        for r in range(groups):
            here = rho[gas_at, TOP + 8 * r:TOP + 8 * r + 8, :]
            up = jnp.where(lanes < cells - 1, pltpu.roll(here, cells - 1, 1), here)
            low = jnp.where(lanes >= 1, pltpu.roll(here, 1, 1), here)
            push[0, 8 * r:8 * r + 8, :] = (up - low) * (0.5 / here)

        for halo in azi_halos(step) + rho_halos(step):
            halo.wait_recv()
        for side, (far, near) in enumerate(beyond):
            for f in range(fluids):
                rho[f, far:far + 1, :] = rho_recv[step, side, f:f + 1, :]
                rho[f, near:near + 1, :] = rho_recv[step, side, fluids + f:fluids + f + 1, :]
                azi[f, near:near + 1, :] = azi_recv[step, side, f:f + 1, :]

        def azimuthal(f, carry):
            for r in range(groups):
                at = TOP + 8 * r
                here = rho[f, at:at + 8, :]
                back_two = rho[f, at - 2:at + 6, :]
                back = rho[f, at - 1:at + 7, :]
                ahead = rho[f, at + 1:at + 9, :]
                ahead_two = rho[f, at + 2:at + 10, :]
                speed = azi[f, at:at + 8, :]
                low = speed + azi[f, at - 1:at + 7, :]
                high = speed + azi[f, at + 1:at + 9, :]
                after = high * jnp.where(high > 0.0, 3.0 * here - back, 3.0 * ahead - ahead_two)
                before = low * jnp.where(low > 0.0, 3.0 * back - back_two, 3.0 * here - ahead)
                div[f, 8 * r:8 * r + 8, :] += after - before
            return carry

        lax.fori_loop(0, fluids, azimuthal, 0)
        for r in range(groups):
            at = TOP + 8 * r
            push[1, 8 * r:8 * r + 8, :] = (
                rho[gas_at, at + 1:at + 9, :] - rho[gas_at, at - 1:at + 7, :]
            ) * (0.5 / rho[gas_at, at:at + 8, :])

        top_all_two().wait_recv()
        for i in range(n - 1):
            top = jnp.maximum(top, top_two[step, i])
        fastest = jnp.max(jnp.max(top, axis=0, keepdims=True), axis=1, keepdims=True)
        dt = courant / (sound_speed + fastest)
        dt_quarter = 0.25 * dt

        def place(chunk, h):
            r = chunk // spans
            start = width * lax.rem(chunk, spans) + span * h
            return (pl.ds(pl.multiple_of(TOP + 8 * r, 8), 8),
                    pl.ds(pl.multiple_of(8 * r, 8), 8),
                    pl.ds(pl.multiple_of(start, 128), span))

        def drag(chunk, h):
            rows, inner, cols = place(chunk, h)
            new_gas = rho[gas_at, rows, cols] - dt_quarter * div[gas_at, inner, cols]
            rho[gas_at, rows, cols] = new_gas
            sums = [jnp.zeros((8, span), jnp.float32)] * 3
            for k in range(local_species):
                scale = dt * inv_stop[k]
                new = rho[k, rows, cols] - dt_quarter * div[k, inner, cols]
                rho[k, rows, cols] = new
                factor = 1.0 / (1.0 + scale * new_gas)
                damp[k, inner, cols] = factor
                weight = (new * factor) * (scale * (1.0 / total_species))
                sums[0] = sums[0] + weight
                sums[1] = sums[1] + weight * rad[k, rows, cols]
                sums[2] = sums[2] + weight * azi[k, rows, cols]
            return sums

        def farther(i):
            return lax.rem(chip + 1 + (chips // 2 - 1 + i) % (chips - 1), chips)

        def sib_copy(z, h):
            return copy_to(terms.at[step, 1 - core, z, h], sib_recv.at[step, z, h],
                           sib_sems.at[step, 0, 0, 0], sib_sems.at[step, 1, z, h],
                           (me_space, sibling))

        def rs_copy(z, h):
            slot = lax.rem(z + chips - 1 - chip, chips)
            return copy_to(terms.at[step, core, z, h], rs_recv.at[step, h, slot],
                           rs_sems.at[step, 0, 0], rs_sems.at[step, 1, h],
                           (me_space, 2 * z + core))

        def rs_all(h):
            return copy_to(rs_recv.at[step, h], rs_recv.at[step, h], rs_sems.at[step, 0, 0],
                           rs_sems.at[step, 1, h], (me_space, sibling))

        def rs_sent():
            return copy_to(rs_recv.at[step], rs_recv.at[step], rs_sems.at[step, 0, 0],
                           rs_sems.at[step, 1, 0], (me_space, sibling))

        def sib_sent():
            held = terms.at[step, 1 - core]
            return copy_to(held, held, sib_sems.at[step, 0, 0, 0], sib_sems.at[step, 1, 0, 0],
                           (me_space, sibling))

        def ag_sent():
            held = gnew.at[step, pl.ds(0, chips - 1)]
            return copy_to(held, held, ag_sems.at[step, 0, 0, 0], ag_sems.at[step, 1, 0, 0],
                           (me_space, sibling))

        def fw_sent():
            held = gnew.at[step, pl.ds(0, chips)]
            return copy_to(held, held, fw_sems.at[step, 0, 0, 0], fw_sems.at[step, 1, 0, 0],
                           (me_space, sibling))

        def ag_copy(z, h):
            return copy_to(gnew.at[step, me, h], gnew.at[step, me, h], ag_sems.at[step, 0, 0, 0],
                           ag_sems.at[step, 1, chip, h], (me_space, 2 * z + core))

        def ag_arrival(z, h):
            there = 2 * z + core
            return copy_to(gnew.at[step, there, h], gnew.at[step, there, h],
                           ag_sems.at[step, 0, 0, 0], ag_sems.at[step, 1, z, h],
                           (me_space, there))

        def fw_copy(z, h):
            there = 2 * z + core
            return copy_to(gnew.at[step, there, h], gnew.at[step, there, h],
                           fw_sems.at[step, 0, 0, 0], fw_sems.at[step, 1, z, h],
                           (me_space, sibling))

        def fw_arrival(z, h):
            there = 2 * z + 1 - core
            return copy_to(gnew.at[step, there, h], gnew.at[step, there, h],
                           fw_sems.at[step, 0, 0, 0], fw_sems.at[step, 1, z, h],
                           (me_space, sibling))

        own = []
        for h in range(halves):
            def for_sibling(z):
                sums = drag(2 * z + 1 - core, h)
                for part in range(3):
                    terms[step, 1 - core, z, h, part] = sums[part]
                sib_copy(z, h).start()

            def for_sibling_step(i, carry):
                for_sibling(farther(i))
                return carry

            loop(chips - 1, for_sibling_step, 0)
            for_sibling(chip)

            def for_peers(i, carry):
                z = farther(i)
                sums = drag(2 * z + core, h)
                sib_copy(z, h).wait_recv()
                for part in range(3):
                    terms[step, core, z, h, part] = sums[part] + sib_recv[step, z, h, part]
                rs_copy(z, h).start()
                return carry

            loop(chips - 1, for_peers, 0)
            own.append(drag(me, h))

        if step + 1 < STEPS:
            send_rho(step + 1)

        for h in range(halves):
            sib_copy(chip, h).wait_recv()

            sums = [own[h][part] + sib_recv[step, chip, h, part] for part in range(3)]
            rs_all(h).wait_recv()
            for i in range(chips - 1):
                sums = [sums[part] + rs_recv[step, h, i, part] for part in range(3)]
            rows, inner, cols = place(me, h)
            inverse = 1.0 / (1.0 + sums[0])
            gnew[step, me, h, 0] = (
                rad[gas_at, rows, cols] - dt * push[0, inner, cols] + sums[1]) * inverse
            gnew[step, me, h, 1] = (
                azi[gas_at, rows, cols] - dt * push[1, inner, cols] + sums[2]) * inverse

            def start_ag(i, carry):
                ag_copy(farther(i), h).start()
                return carry

            loop(chips - 1, start_ag, 0)
            fw_copy(chip, h).start()

        def update(chunk, h, best):
            rows, inner, cols = place(chunk, h)
            gas_rad = gnew[step, chunk, h, 0]
            gas_azi = gnew[step, chunk, h, 1]
            rad[gas_at, rows, cols] = gas_rad
            azi[gas_at, rows, cols] = gas_azi
            if step == STEPS - 1:
                return best
            speed = jnp.abs(gas_rad) + jnp.abs(gas_azi)
            for k in range(local_species):
                factor = damp[k, inner, cols]
                new_rad = gas_rad + (rad[k, rows, cols] - gas_rad) * factor
                new_azi = gas_azi + (azi[k, rows, cols] - gas_azi) * factor
                rad[k, rows, cols] = new_rad
                azi[k, rows, cols] = new_azi
                speed = jnp.maximum(speed, jnp.abs(new_rad) + jnp.abs(new_azi))
            return jnp.maximum(best, fold(speed))

        top = jnp.zeros((8, 128), jnp.float32)
        for h in range(halves):
            top = update(me, h, top)

            def update_peer(i, best):
                z = lax.rem(chip + 1 + i, chips)
                ag_arrival(z, h).wait_recv()
                fw_copy(z, h).start()
                return update(2 * z + core, h, best)

            top = loop(chips - 1, update_peer, top)

            def update_sibling(i, best):
                z = lax.rem(chip + i, chips)
                fw_arrival(z, h).wait_recv()
                return update(2 * z + 1 - core, h, best)

            top = loop(chips, update_sibling, top)

        unsent.append((top_all_one(), top_all_two(), sib_sent(), rs_sent(), ag_sent(), fw_sent(),
                       *rho_halos(step), *azi_halos(step)))
        return top

    for step in range(STEPS):
        top = run_step(step, top)

    for sends in unsent:
        for send in sends:
            send.wait_send()


def finish(rho, rad, azi, damp, dust_out, gas_out, new, sems):
    local_species, tile_rows, _ = damp.shape
    interior = pl.ds(TOP, tile_rows)
    copies = [pltpu.make_async_copy(
        rho.at[pl.ds(0, local_species), interior], dust_out.at[0], sems.at[0])]
    for part, held in enumerate((rho, rad, azi)):
        copies.append(pltpu.make_async_copy(
            held.at[local_species, interior], gas_out.at[part], sems.at[1 + part]))
    for copy in copies:
        copy.start()
    for k in range(local_species):
        for r in range(tile_rows // 8):
            rows = slice(TOP + 8 * r, TOP + 8 * r + 8)
            inner = slice(8 * r, 8 * r + 8)
            factor = damp[k, inner, :]
            for part, held in enumerate((rad, azi)):
                gas = held[local_species, rows, :]
                new[part, k, inner, :] = gas + (held[k, rows, :] - gas) * factor
        for part in range(2):
            copy = pltpu.make_async_copy(
                new.at[part, k], dust_out.at[part + 1, k], sems.at[4 + 2 * k + part])
            copy.start()
            copies.append(copy)
    for copy in copies:
        copy.wait()


def solution(mesh):
    n = mesh.shape["species"]
    m = mesh.shape["space"]

    def local(dust_state, gas_state, species_bin):
        local_species, tile_rows, cells = dust_state.shape[1:]
        fluids = local_species + 1
        groups = tile_rows // 8
        width = cells // (n // groups)
        halves = min(HALVES, width // 128)
        span = width // halves
        chips = n // 2
        f32 = jnp.float32
        rho_rows = -(-2 * fluids // 8) * 8
        azi_rows = -(-fluids // 8) * 8
        extended = pltpu.VMEM((fluids, tile_rows + 16, cells), f32)
        damped = pltpu.VMEM((local_species, tile_rows, cells), f32)
        dma = pltpu.SemaphoreType.DMA
        near = pl.BlockSpec(memory_space=pltpu.VMEM)
        far = pl.BlockSpec(memory_space=pltpu.HBM)
        held = pl.pallas_call(
            functools.partial(kernel, n, m),
            out_shape=(extended, extended, extended, damped),
            in_specs=[far, far, far],
            out_specs=(near,) * 4,
            scratch_shapes=[
                pltpu.SMEM((local_species,), jnp.int32),
                pltpu.VMEM((fluids, tile_rows, cells), f32),
                pltpu.VMEM((2, tile_rows, cells), f32),
                pltpu.VMEM((STEPS, 2, chips, halves, 3, 8, span), f32),
                pltpu.VMEM((STEPS, n, halves, 2, 8, span), f32),
                pltpu.VMEM((STEPS, chips, halves, 3, 8, span), f32),
                pltpu.VMEM((STEPS, halves, chips - 1, 3, 8, span), f32),
                pltpu.VMEM((STEPS, 8, 128), f32),
                pltpu.VMEM((STEPS, m - 1, 8, 128), f32),
                pltpu.VMEM((STEPS, 8, 128), f32),
                pltpu.VMEM((STEPS, n - 1, 8, 128), f32),
                pltpu.VMEM((STEPS, 2, rho_rows, cells), f32),
                pltpu.VMEM((STEPS, 2, rho_rows, cells), f32),
                pltpu.VMEM((STEPS, 2, azi_rows, cells), f32),
                pltpu.VMEM((STEPS, 2, azi_rows, cells), f32),
                dma((7,)),
                dma((STEPS, 4)),
                dma((STEPS, 4, 2)),
                dma((STEPS, 2, chips, halves)),
                dma((STEPS, 2, halves)),
                dma((STEPS, 2, chips, halves)),
                dma((STEPS, 2, chips, halves)),
            ],
            compiler_params=pltpu.CompilerParams(
                collective_id=0, has_side_effects=True, vmem_limit_bytes=58 * 1024 * 1024),
            cost_estimate=pl.CostEstimate(
                flops=200 * fluids * tile_rows * cells,
                bytes_accessed=24 * fluids * tile_rows * cells, transcendentals=0),
            name="disk_steps",
        )(dust_state, gas_state, species_bin)
        return pl.pallas_call(
            finish,
            out_shape=(jax.ShapeDtypeStruct(dust_state.shape, f32),
                       jax.ShapeDtypeStruct(gas_state.shape, f32)),
            in_specs=[near] * 4,
            out_specs=(far, far),
            scratch_shapes=[
                pltpu.VMEM((2, local_species, tile_rows, cells), f32),
                dma((4 + 2 * local_species,)),
            ],
            compiler_params=pltpu.CompilerParams(vmem_limit_bytes=20 * 1024 * 1024),
            name="last_update",
        )(*held)

    return jax.shard_map(
        local,
        mesh=mesh,
        in_specs=(P(None, "species", "space", None), P(None, "space", None), P("species")),
        out_specs=(P(None, "species", "space", None), P(None, "space", None)),
        check_vma=False,
    )
```

```python
import functools

import jax
import jax.numpy as jnp
from jax import lax
from jax.experimental import pallas as pl
from jax.experimental.pallas import tpu as pltpu
from jax.sharding import PartitionSpec as P

STEPS = 2

courant = 0.25
sound_speed = 1.0
stop_floor = 0.003
stop_span = 6.907755

MESH = pl.DeviceIdType.MESH
TOP = 8
HALVES = 2


def loop(count, body, carry):
    if count > 8:
        return lax.fori_loop(0, count, body, carry)
    for i in range(count):
        carry = body(i, carry)
    return carry


def kernel(
    n, m, dust, gas, species_bins, rho, rad, azi, damp,
    species_bin, div, push, terms, gnew,
    sib_recv, rs_recv, top_send, top_one, top_mid, top_two, rho_send, rho_recv, azi_send, azi_recv,
    io_sem, top_sems, halo_sems, sib_sems, rs_sems, ag_sems, fw_sems,
):
    local_species, tile_rows, cells = dust.shape[1:]
    fluids = local_species + 1
    gas_at = local_species
    groups = tile_rows // 8
    spans = n // groups
    width = cells // spans
    halves = min(HALVES, width // 128)
    span = width // halves
    chips = n // 2
    total_species = local_species * n
    bottom = TOP + tile_rows

    me_space = lax.axis_index("space")
    me = lax.axis_index("species")
    core = lax.rem(me, 2)
    chip = me // 2
    sibling = me + 1 - 2 * core
    interior = pl.ds(TOP, tile_rows)

    barrier = pltpu.get_barrier_semaphore()

    def greet_species(i, carry):
        pl.semaphore_signal(
            barrier, inc=1, device_id=(me_space, lax.rem(me + 1 + i, n)), device_id_type=MESH)
        return carry

    def greet_space(i, carry):
        pl.semaphore_signal(
            barrier, inc=1, device_id=(lax.rem(me_space + 1 + i, m), me), device_id_type=MESH)
        return carry

    loop(n - 1, greet_species, 0)
    loop(m - 1, greet_space, 0)
    loads = []
    for part, held in enumerate((rho, rad, azi)):
        loads.append(pltpu.make_async_copy(
            dust.at[part], held.at[pl.ds(0, local_species), interior], io_sem.at[2 * part]))
        loads.append(pltpu.make_async_copy(
            gas.at[part], held.at[gas_at, interior], io_sem.at[2 * part + 1]))
    loads.append(pltpu.make_async_copy(species_bins, species_bin, io_sem.at[6]))
    for load in loads:
        load.start()
    for load in loads:
        load.wait()

    def fold(values):
        best = values[:, :128]
        for start in range(128, values.shape[1], 128):
            best = jnp.maximum(best, values[:, start:start + 128])
        return best

    def first_top(f, best):
        for at in range(TOP, bottom, 8):
            best = jnp.maximum(
                best, fold(jnp.abs(rad[f, at:at + 8, :]) + jnp.abs(azi[f, at:at + 8, :])))
        return best

    top = lax.fori_loop(0, fluids, first_top, jnp.zeros((8, 128), jnp.float32))

    def copy_to(src, dst, send, recv, where):
        return pltpu.make_async_remote_copy(
            src_ref=src, dst_ref=dst, send_sem=send, recv_sem=recv,
            device_id=where, device_id_type=MESH)

    inv_stop = [
        jnp.exp(jnp.full((1, 1), species_bin[k].astype(jnp.float32))
                * (-stop_span / (total_species - 1))) * (1.0 / stop_floor)
        for k in range(local_species)]
    lanes = lax.broadcasted_iota(jnp.int32, (8, cells), 1)

    neighbours = (lax.rem(me_space + 1, m), lax.rem(me_space + m - 1, m))
    edges = ((bottom - 2, bottom - 1), (TOP + 1, TOP))
    beyond = ((TOP - 2, TOP - 1), (bottom + 1, bottom))

    def rho_halos(step):
        return [copy_to(rho_send.at[step, side], rho_recv.at[step, side],
                        halo_sems.at[step, 0, side], halo_sems.at[step, 1, side], (there, me))
                for side, there in enumerate(neighbours)]

    def azi_halos(step):
        return [copy_to(azi_send.at[step, side], azi_recv.at[step, side],
                        halo_sems.at[step, 2, side], halo_sems.at[step, 3, side], (there, me))
                for side, there in enumerate(neighbours)]

    def send_rho(step):
        for side, (far, near) in enumerate(edges):
            for f in range(fluids):
                rho_send[step, side, f:f + 1, :] = rho[f, far:far + 1, :]
                rho_send[step, side, fluids + f:fluids + f + 1, :] = rho[f, near:near + 1, :]
        for halo in rho_halos(step):
            halo.start()

    def send_azi(step):
        for side, (_, near) in enumerate(edges):
            for f in range(fluids):
                azi_send[step, side, f:f + 1, :] = azi[f, near:near + 1, :]
        for halo in azi_halos(step):
            halo.start()

    unsent = []

    def run_step(step, top):
        top_send[step] = top
        if step == 0:
            pl.semaphore_wait(barrier, n + m - 2)

        def top_copy_one(i):
            there = lax.rem(me_space + 1 + i, m)
            return copy_to(top_send.at[step], top_one.at[step, i], top_sems.at[step, 0],
                           top_sems.at[step, 1], (there, me))

        def top_copy_two(i):
            there = lax.rem(me + 1 + i, n)
            return copy_to(top_mid.at[step], top_two.at[step, i], top_sems.at[step, 2],
                           top_sems.at[step, 3], (me_space, there))

        def top_all_one():
            return copy_to(top_one.at[step], top_one.at[step], top_sems.at[step, 0],
                           top_sems.at[step, 1], (neighbours[0], me))

        def top_all_two():
            return copy_to(top_two.at[step], top_two.at[step], top_sems.at[step, 2],
                           top_sems.at[step, 3], (me_space, sibling))

        def start_one(i, carry):
            top_copy_one(i).start()
            return carry

        loop(m - 1, start_one, 0)
        send_azi(step)
        if step == 0:
            send_rho(step)

        def radial(f, carry):
            for r in range(groups):
                here = rho[f, TOP + 8 * r:TOP + 8 * r + 8, :]
                speed = rad[f, TOP + 8 * r:TOP + 8 * r + 8, :]
                back = jnp.where(lanes >= 1, pltpu.roll(here, 1, 1), 0.0)
                ahead = jnp.where(lanes < cells - 1, pltpu.roll(here, cells - 1, 1), 0.0)
                down = 3.0 * here - ahead
                down_next = jnp.where(lanes < cells - 1, pltpu.roll(down, cells - 1, 1), 0.0)
                face = speed + jnp.where(
                    lanes < cells - 1, pltpu.roll(speed, cells - 1, 1), 0.0)
                flux = face * jnp.where(face > 0.0, 3.0 * here - back, down_next)
                before = jnp.where(
                    lanes >= 1, pltpu.roll(flux, 1, 1), jnp.minimum(speed, 0.0) * down)
                div[f, 8 * r:8 * r + 8, :] = flux - before
            return carry

        early = fluids * 2 // 5
        lax.fori_loop(0, early, radial, 0)

        top_all_one().wait_recv()
        for i in range(m - 1):
            top = jnp.maximum(top, top_one[step, i])
        top_mid[step] = top

        def start_two(i, carry):
            top_copy_two(i).start()
            return carry

        loop(n - 1, start_two, 0)

        lax.fori_loop(early, fluids, radial, 0)
        for r in range(groups):
            here = rho[gas_at, TOP + 8 * r:TOP + 8 * r + 8, :]
            up = jnp.where(lanes < cells - 1, pltpu.roll(here, cells - 1, 1), here)
            low = jnp.where(lanes >= 1, pltpu.roll(here, 1, 1), here)
            push[0, 8 * r:8 * r + 8, :] = (up - low) * (0.5 / here)

        for halo in azi_halos(step) + rho_halos(step):
            halo.wait_recv()
        for side, (far, near) in enumerate(beyond):
            for f in range(fluids):
                rho[f, far:far + 1, :] = rho_recv[step, side, f:f + 1, :]
                rho[f, near:near + 1, :] = rho_recv[step, side, fluids + f:fluids + f + 1, :]
                azi[f, near:near + 1, :] = azi_recv[step, side, f:f + 1, :]

        def azimuthal(f, carry):
            for r in range(groups):
                at = TOP + 8 * r
                here = rho[f, at:at + 8, :]
                back_two = rho[f, at - 2:at + 6, :]
                back = rho[f, at - 1:at + 7, :]
                ahead = rho[f, at + 1:at + 9, :]
                ahead_two = rho[f, at + 2:at + 10, :]
                speed = azi[f, at:at + 8, :]
                low = speed + azi[f, at - 1:at + 7, :]
                high = speed + azi[f, at + 1:at + 9, :]
                after = high * jnp.where(high > 0.0, 3.0 * here - back, 3.0 * ahead - ahead_two)
                before = low * jnp.where(low > 0.0, 3.0 * back - back_two, 3.0 * here - ahead)
                div[f, 8 * r:8 * r + 8, :] += after - before
            return carry

        lax.fori_loop(0, fluids, azimuthal, 0)
        for r in range(groups):
            at = TOP + 8 * r
            push[1, 8 * r:8 * r + 8, :] = (
                rho[gas_at, at + 1:at + 9, :] - rho[gas_at, at - 1:at + 7, :]
            ) * (0.5 / rho[gas_at, at:at + 8, :])

        top_all_two().wait_recv()
        for i in range(n - 1):
            top = jnp.maximum(top, top_two[step, i])
        fastest = jnp.max(jnp.max(top, axis=0, keepdims=True), axis=1, keepdims=True)
        dt = courant / (sound_speed + fastest)
        dt_quarter = 0.25 * dt

        def place(chunk, h):
            r = chunk // spans
            start = width * lax.rem(chunk, spans) + span * h
            return (pl.ds(pl.multiple_of(TOP + 8 * r, 8), 8),
                    pl.ds(pl.multiple_of(8 * r, 8), 8),
                    pl.ds(pl.multiple_of(start, 128), span))

        def drag(chunk, h):
            rows, inner, cols = place(chunk, h)
            new_gas = rho[gas_at, rows, cols] - dt_quarter * div[gas_at, inner, cols]
            rho[gas_at, rows, cols] = new_gas
            sums = [jnp.zeros((8, span), jnp.float32)] * 3
            for k in range(local_species):
                scale = dt * inv_stop[k]
                new = rho[k, rows, cols] - dt_quarter * div[k, inner, cols]
                rho[k, rows, cols] = new
                factor = 1.0 / (1.0 + scale * new_gas)
                damp[k, inner, cols] = factor
                weight = (new * factor) * (scale * (1.0 / total_species))
                sums[0] = sums[0] + weight
                sums[1] = sums[1] + weight * rad[k, rows, cols]
                sums[2] = sums[2] + weight * azi[k, rows, cols]
            return sums

        def farther(i):
            return lax.rem(chip + 1 + (chips // 2 - 1 + i) % (chips - 1), chips)

        def sib_copy(z, h):
            return copy_to(terms.at[step, 1 - core, z, h], sib_recv.at[step, z, h],
                           sib_sems.at[step, 0, 0, 0], sib_sems.at[step, 1, z, h],
                           (me_space, sibling))

        def rs_copy(z, h):
            slot = lax.rem(z + chips - 1 - chip, chips)
            return copy_to(terms.at[step, core, z, h], rs_recv.at[step, h, slot],
                           rs_sems.at[step, 0, 0], rs_sems.at[step, 1, h],
                           (me_space, 2 * z + core))

        def rs_all(h):
            return copy_to(rs_recv.at[step, h], rs_recv.at[step, h], rs_sems.at[step, 0, 0],
                           rs_sems.at[step, 1, h], (me_space, sibling))

        def rs_sent():
            return copy_to(rs_recv.at[step], rs_recv.at[step], rs_sems.at[step, 0, 0],
                           rs_sems.at[step, 1, 0], (me_space, sibling))

        def sib_sent():
            held = terms.at[step, 1 - core]
            return copy_to(held, held, sib_sems.at[step, 0, 0, 0], sib_sems.at[step, 1, 0, 0],
                           (me_space, sibling))

        def ag_sent():
            held = gnew.at[step, pl.ds(0, chips - 1)]
            return copy_to(held, held, ag_sems.at[step, 0, 0, 0], ag_sems.at[step, 1, 0, 0],
                           (me_space, sibling))

        def fw_sent():
            held = gnew.at[step, pl.ds(0, chips)]
            return copy_to(held, held, fw_sems.at[step, 0, 0, 0], fw_sems.at[step, 1, 0, 0],
                           (me_space, sibling))

        def ag_copy(z, h):
            return copy_to(gnew.at[step, me, h], gnew.at[step, me, h], ag_sems.at[step, 0, 0, 0],
                           ag_sems.at[step, 1, chip, h], (me_space, 2 * z + core))

        def ag_arrival(z, h):
            there = 2 * z + core
            return copy_to(gnew.at[step, there, h], gnew.at[step, there, h],
                           ag_sems.at[step, 0, 0, 0], ag_sems.at[step, 1, z, h],
                           (me_space, there))

        def fw_copy(z, h):
            there = 2 * z + core
            return copy_to(gnew.at[step, there, h], gnew.at[step, there, h],
                           fw_sems.at[step, 0, 0, 0], fw_sems.at[step, 1, z, h],
                           (me_space, sibling))

        def fw_arrival(z, h):
            there = 2 * z + 1 - core
            return copy_to(gnew.at[step, there, h], gnew.at[step, there, h],
                           fw_sems.at[step, 0, 0, 0], fw_sems.at[step, 1, z, h],
                           (me_space, sibling))

        own = []
        for h in range(halves):
            def for_sibling(z):
                sums = drag(2 * z + 1 - core, h)
                for part in range(3):
                    terms[step, 1 - core, z, h, part] = sums[part]
                sib_copy(z, h).start()

            def for_sibling_step(i, carry):
                for_sibling(farther(i))
                return carry

            loop(chips - 1, for_sibling_step, 0)
            for_sibling(chip)

            def for_peers(i, carry):
                z = farther(i)
                sums = drag(2 * z + core, h)
                sib_copy(z, h).wait_recv()
                for part in range(3):
                    terms[step, core, z, h, part] = sums[part] + sib_recv[step, z, h, part]
                rs_copy(z, h).start()
                return carry

            loop(chips - 1, for_peers, 0)
            own.append(drag(me, h))

        if step + 1 < STEPS:
            send_rho(step + 1)

        for h in range(halves):
            sib_copy(chip, h).wait_recv()

            sums = [own[h][part] + sib_recv[step, chip, h, part] for part in range(3)]
            rs_all(h).wait_recv()
            for i in range(chips - 1):
                sums = [sums[part] + rs_recv[step, h, i, part] for part in range(3)]
            rows, inner, cols = place(me, h)
            inverse = 1.0 / (1.0 + sums[0])
            gnew[step, me, h, 0] = (
                rad[gas_at, rows, cols] - dt * push[0, inner, cols] + sums[1]) * inverse
            gnew[step, me, h, 1] = (
                azi[gas_at, rows, cols] - dt * push[1, inner, cols] + sums[2]) * inverse

            def start_ag(i, carry):
                ag_copy(farther(i), h).start()
                return carry

            loop(chips - 1, start_ag, 0)
            fw_copy(chip, h).start()

        def update(chunk, h, best):
            rows, inner, cols = place(chunk, h)
            gas_rad = gnew[step, chunk, h, 0]
            gas_azi = gnew[step, chunk, h, 1]
            rad[gas_at, rows, cols] = gas_rad
            azi[gas_at, rows, cols] = gas_azi
            if step == STEPS - 1:
                return best
            speed = jnp.abs(gas_rad) + jnp.abs(gas_azi)
            for k in range(local_species):
                factor = damp[k, inner, cols]
                new_rad = gas_rad + (rad[k, rows, cols] - gas_rad) * factor
                new_azi = gas_azi + (azi[k, rows, cols] - gas_azi) * factor
                rad[k, rows, cols] = new_rad
                azi[k, rows, cols] = new_azi
                speed = jnp.maximum(speed, jnp.abs(new_rad) + jnp.abs(new_azi))
            return jnp.maximum(best, fold(speed))

        top = jnp.zeros((8, 128), jnp.float32)
        for h in range(halves):
            top = update(me, h, top)

            def update_peer(i, best):
                z = lax.rem(chip + 1 + i, chips)
                ag_arrival(z, h).wait_recv()
                fw_copy(z, h).start()
                return update(2 * z + core, h, best)

            top = loop(chips - 1, update_peer, top)

            def update_sibling(i, best):
                z = lax.rem(chip + i, chips)
                fw_arrival(z, h).wait_recv()
                return update(2 * z + 1 - core, h, best)

            top = loop(chips, update_sibling, top)

        unsent.append((top_all_one(), top_all_two(), sib_sent(), rs_sent(), ag_sent(), fw_sent(),
                       *rho_halos(step), *azi_halos(step)))
        return top

    for step in range(STEPS):
        top = run_step(step, top)

    for sends in unsent:
        for send in sends:
            send.wait_send()


def finish(rho, rad, azi, damp, dust_out, gas_out, new, sems):
    local_species, tile_rows, _ = damp.shape
    interior = pl.ds(TOP, tile_rows)
    copies = [pltpu.make_async_copy(
        rho.at[pl.ds(0, local_species), interior], dust_out.at[0], sems.at[0])]
    for part, held in enumerate((rho, rad, azi)):
        copies.append(pltpu.make_async_copy(
            held.at[local_species, interior], gas_out.at[part], sems.at[1 + part]))
    for copy in copies:
        copy.start()
    for k in range(local_species):
        for r in range(tile_rows // 8):
            rows = slice(TOP + 8 * r, TOP + 8 * r + 8)
            inner = slice(8 * r, 8 * r + 8)
            factor = damp[k, inner, :]
            for part, held in enumerate((rad, azi)):
                gas = held[local_species, rows, :]
                new[part, k, inner, :] = gas + (held[k, rows, :] - gas) * factor
        for part in range(2):
            copy = pltpu.make_async_copy(
                new.at[part, k], dust_out.at[part + 1, k], sems.at[4 + 2 * k + part])
            copy.start()
            copies.append(copy)
    for copy in copies:
        copy.wait()


def solution(mesh):
    n = mesh.shape["species"]
    m = mesh.shape["space"]

    def local(dust_state, gas_state, species_bin):
        local_species, tile_rows, cells = dust_state.shape[1:]
        fluids = local_species + 1
        groups = tile_rows // 8
        width = cells // (n // groups)
        halves = min(HALVES, width // 128)
        span = width // halves
        chips = n // 2
        f32 = jnp.float32
        rho_rows = -(-2 * fluids // 8) * 8
        azi_rows = -(-fluids // 8) * 8
        extended = pltpu.VMEM((fluids, tile_rows + 16, cells), f32)
        damped = pltpu.VMEM((local_species, tile_rows, cells), f32)
        dma = pltpu.SemaphoreType.DMA
        near = pl.BlockSpec(memory_space=pltpu.VMEM)
        far = pl.BlockSpec(memory_space=pltpu.HBM)
        held = pl.pallas_call(
            functools.partial(kernel, n, m),
            out_shape=(extended, extended, extended, damped),
            in_specs=[far, far, far],
            out_specs=(near,) * 4,
            scratch_shapes=[
                pltpu.SMEM((local_species,), jnp.int32),
                pltpu.VMEM((fluids, tile_rows, cells), f32),
                pltpu.VMEM((2, tile_rows, cells), f32),
                pltpu.VMEM((STEPS, 2, chips, halves, 3, 8, span), f32),
                pltpu.VMEM((STEPS, n, halves, 2, 8, span), f32),
                pltpu.VMEM((STEPS, chips, halves, 3, 8, span), f32),
                pltpu.VMEM((STEPS, halves, chips - 1, 3, 8, span), f32),
                pltpu.VMEM((STEPS, 8, 128), f32),
                pltpu.VMEM((STEPS, m - 1, 8, 128), f32),
                pltpu.VMEM((STEPS, 8, 128), f32),
                pltpu.VMEM((STEPS, n - 1, 8, 128), f32),
                pltpu.VMEM((STEPS, 2, rho_rows, cells), f32),
                pltpu.VMEM((STEPS, 2, rho_rows, cells), f32),
                pltpu.VMEM((STEPS, 2, azi_rows, cells), f32),
                pltpu.VMEM((STEPS, 2, azi_rows, cells), f32),
                dma((7,)),
                dma((STEPS, 4)),
                dma((STEPS, 4, 2)),
                dma((STEPS, 2, chips, halves)),
                dma((STEPS, 2, halves)),
                dma((STEPS, 2, chips, halves)),
                dma((STEPS, 2, chips, halves)),
            ],
            compiler_params=pltpu.CompilerParams(
                collective_id=0, has_side_effects=True, vmem_limit_bytes=58 * 1024 * 1024),
            cost_estimate=pl.CostEstimate(
                flops=200 * fluids * tile_rows * cells,
                bytes_accessed=24 * fluids * tile_rows * cells, transcendentals=0),
            name="disk_steps",
        )(dust_state, gas_state, species_bin)
        return pl.pallas_call(
            finish,
            out_shape=(jax.ShapeDtypeStruct(dust_state.shape, f32),
                       jax.ShapeDtypeStruct(gas_state.shape, f32)),
            in_specs=[near] * 4,
            out_specs=(far, far),
            scratch_shapes=[
                pltpu.VMEM((2, local_species, tile_rows, cells), f32),
                dma((4 + 2 * local_species,)),
            ],
            compiler_params=pltpu.CompilerParams(vmem_limit_bytes=20 * 1024 * 1024),
            name="last_update",
        )(*held)

    return jax.shard_map(
        local,
        mesh=mesh,
        in_specs=(P(None, "species", "space", None), P(None, "space", None), P("species")),
        out_specs=(P(None, "species", "space", None), P(None, "space", None)),
        check_vma=False,
    )
```
